32 devices in a mesh: gx: 4 (over y, core), gy: 2 (over x), gz: 4 (over z).
Axes of the slice: x: 2, y: 2, z: 4, core: 2. Of those that a mesh axis runs over, the one named last changes fastest.
Arguments:
- tokens: bfloat16 [32, 16, 32, 256], P('gx', 'gy', 'gz'), may hold values from -6 to 6
- norm_gain: float32 [256], replicated, may hold values from 0.5 to 1.5
- query_weight: bfloat16 [256, 256], replicated, may hold values from -2 to 2
- key_weight: bfloat16 [256, 256], replicated, may hold values from -2 to 2
- value_weight: bfloat16 [256, 256], replicated, may hold values from -0.375 to 0.375
- head_scale: float32 [8], replicated, may hold values from 1 to 6
- out_weight: bfloat16 [256, 256], replicated, may hold values from -0.375 to 0.375
- mlp_gain: float32 [256], replicated, may hold values from 0.5 to 1.5
- up_weight: bfloat16 [256, 512], replicated, may hold values from -0.375 to 0.375
- down_weight: bfloat16 [512, 256], replicated, may hold values from -0.25 to 0.25
Outputs:
- layer_out: bfloat16 [32, 16, 32, 256], P('gx', 'gy', 'gz')
The draws below stay inside these ranges and needn't reach their ends.
All inputs are finite; a program needn't handle non-finite values.
Results may differ from the reference program's by a relative error of at most 0.0095.
Values may be sent and summed in bfloat16 or wider, within the bound.
No kernel may reach another device: no remote copies, remote signals or barrier semaphores. Data moves between devices by JAX's collectives and lax.ppermute only.
A program may use at most 128 MiB of HBM per device.

```python
import math
import jax
import jax.numpy as jnp
from jax import lax

C = 256
HEADS = 8
HID = 512
TOK_DEV = 512
NX = 32
NY = 16
NZ = 32


def draw_key_weight(key, part):
    values = jax.random.normal(jax.random.fold_in(key, 21), (C, C), jnp.float32) / math.sqrt(C)
    return jnp.clip(values, -2.0, 2.0).astype(jnp.bfloat16)


def draw_query_weight(key, part):
    noise = jax.random.normal(jax.random.fold_in(key, 31), (C, C), jnp.float32) / math.sqrt(C)
    values = noise
    return jnp.clip(values, -2.0, 2.0).astype(jnp.bfloat16)


def draw_tokens(key, part):
    rough = jax.random.normal(jax.random.fold_in(key, 41), (NX, NY, NZ, C), jnp.float32)
    smooth = jax.random.normal(jax.random.fold_in(key, 43), (NX // 4, NY // 4, NZ // 4, C), jnp.float32)
    smooth = jnp.repeat(jnp.repeat(jnp.repeat(smooth, 4, axis=0), 4, axis=1), 4, axis=2)
    values = smooth + rough
    return jnp.clip(values, -6.0, 6.0).astype(jnp.bfloat16)


def normal_values(stream_key, dims, scale, most, held_as=jnp.bfloat16):
    entries = jax.random.normal(stream_key, dims, jnp.float32) * scale
    return jnp.minimum(jnp.maximum(entries, -most), most).astype(held_as)


def setup_inputs(seed: int = 0) -> dict:
    arg_keys = jax.random.split(jax.random.key(seed), 11)
    return {
        "tokens": draw_tokens(jax.random.fold_in(arg_keys[10], 71), 0),
        "norm_gain": jnp.clip(1.0 + 0.1 * jax.random.normal(arg_keys[1], (C,), jnp.float32), 0.5, 1.5),
        "query_weight": draw_query_weight(jax.random.fold_in(arg_keys[10], 71), 0),
        "key_weight": draw_key_weight(jax.random.fold_in(arg_keys[10], 71), 0),
        "value_weight": normal_values(arg_keys[4], (C, C), C ** -0.5, 0.375),
        "head_scale": jnp.clip(jnp.exp(jax.random.uniform(arg_keys[5], (HEADS,), jnp.float32, math.log(1.0), math.log(6.0))), 1.0, 6.0),
        "out_weight": normal_values(arg_keys[6], (C, C), C ** -0.5, 0.375),
        "mlp_gain": jnp.clip(1.0 + 0.1 * jax.random.normal(arg_keys[7], (C,), jnp.float32), 0.5, 1.5),
        "up_weight": normal_values(arg_keys[8], (C, HID), C ** -0.5, 0.375),
        "down_weight": normal_values(arg_keys[9], (HID, C), HID ** -0.5, 0.25),
    }


EPSILON = 1e-05

def layer_norm(values, gain):
    widened = values.astype(jnp.float32)
    average = lax.optimization_barrier(jnp.mean(widened, axis=-1, keepdims=True))
    centered = widened - average
    variance = lax.optimization_barrier(jnp.mean(centered * centered, axis=-1, keepdims=True))
    return (centered * lax.rsqrt(variance + EPSILON) * gain).astype(jnp.bfloat16)

def project(values, weight):
    flat = values.reshape(-1, values.shape[-1])
    result = jnp.dot(flat, weight, preferred_element_type=jnp.float32)
    return result.astype(jnp.bfloat16).reshape(values.shape[:-1] + (weight.shape[1],))

def pooled_mean(values, factor):
    extent = values.shape
    grouped = values.reshape(extent[0] // factor, factor, extent[1] // factor, factor, extent[2] // factor, factor, extent[3])
    return lax.optimization_barrier(jnp.mean(grouped, axis=(1, 3, 5), dtype=jnp.float32)).astype(jnp.bfloat16)

def wrap_pad(values):
    return jnp.pad(values, ((1, 1), (1, 1), (1, 1), (0, 0)), mode='wrap')

def unfold_axis(padded, dimension):
    windows = padded.shape[dimension] // 2 - 1
    paired = padded.reshape(padded.shape[:dimension] + (windows + 1, 2) + padded.shape[dimension + 1:])
    lower = lax.slice_in_dim(paired, 0, windows, axis=dimension)
    upper = lax.slice_in_dim(paired, 1, windows + 1, axis=dimension)
    return jnp.concatenate([lower, upper], axis=dimension + 1)

def unfold(padded):
    for dimension in (0, 2, 4):
        padded = unfold_axis(padded, dimension)
    return padded.transpose(0, 2, 4, 1, 3, 5, 6).reshape(padded.shape[0], padded.shape[2], padded.shape[4], 64, padded.shape[6])

def window_attend(key_pad, value_pad, queries, scaling):
    key_cells = unfold(key_pad)
    value_cells = unfold(value_pad)
    along_x, along_y, along_z, window_size, channels = key_cells.shape
    head_width = channels // HEADS
    query_side = queries.shape[0] // along_x
    windows = along_x * along_y * along_z
    grouped = queries.reshape(along_x, query_side, along_y, query_side, along_z, query_side, channels)
    grouped = grouped.transpose(0, 2, 4, 1, 3, 5, 6).reshape(windows, query_side ** 3, HEADS, head_width)
    key_cells = key_cells.reshape(windows, window_size, HEADS, head_width)
    value_cells = value_cells.reshape(windows, window_size, HEADS, head_width)
    scores = jnp.einsum('wqhd,wkhd->whqk', grouped.astype(jnp.float32), key_cells.astype(jnp.float32)) * scaling[None, :, None, None]
    highest = lax.optimization_barrier(jnp.max(scores, axis=-1, keepdims=True))
    weights = jnp.exp(scores - highest)
    summed = lax.optimization_barrier(jnp.sum(weights, axis=-1, keepdims=True))
    rounded = lax.optimization_barrier(weights.astype(jnp.bfloat16)).astype(jnp.float32)
    blended = jnp.einsum('whqk,wkhd->wqhd', rounded, value_cells.astype(jnp.float32))
    blended = blended / jnp.transpose(summed, (0, 2, 1, 3))
    blended = blended.reshape(along_x, along_y, along_z, query_side, query_side, query_side, channels)
    return blended.transpose(0, 3, 1, 4, 2, 5, 6).reshape(queries.shape)

def level_attend(key_pad, value_pad, queries, scaling):
    window_rows = (key_pad.shape[0] - 2) // 2
    query_side = queries.shape[0] // window_rows

    def one_row(row_index):
        key_slab = lax.dynamic_slice_in_dim(key_pad, (2 * row_index).astype(jnp.int32), 4, 0)
        value_slab = lax.dynamic_slice_in_dim(value_pad, (2 * row_index).astype(jnp.int32), 4, 0)
        query_slab = lax.dynamic_slice_in_dim(queries, (query_side * row_index).astype(jnp.int32), query_side, 0)
        return window_attend(key_slab, value_slab, query_slab, scaling)
    stacked = lax.map(one_row, jnp.arange(window_rows, dtype=jnp.int32))
    return stacked.reshape(queries.shape)

def coarse_attend(query_rows, coarse_keys, coarse_values, scaling):
    channels = query_rows.shape[-1]
    head_width = channels // HEADS
    key_heads = coarse_keys.reshape(-1, HEADS, head_width).astype(jnp.float32)
    value_heads = coarse_values.reshape(-1, HEADS, head_width).astype(jnp.float32)

    def one_block(block_rows):
        query_heads = block_rows.reshape(-1, HEADS, head_width).astype(jnp.float32)
        scores = jnp.einsum('qhd,khd->hqk', query_heads, key_heads) * scaling[:, None, None]
        highest = lax.optimization_barrier(jnp.max(scores, axis=-1, keepdims=True))
        weights = jnp.exp(scores - highest)
        summed = lax.optimization_barrier(jnp.sum(weights, axis=-1, keepdims=True))
        rounded = lax.optimization_barrier(weights.astype(jnp.bfloat16)).astype(jnp.float32)
        blended = jnp.einsum('hqk,khd->qhd', rounded, value_heads) / jnp.transpose(summed, (1, 0, 2))
        return blended.reshape(block_rows.shape)
    stacked = lax.map(one_block, query_rows.reshape(-1, TOK_DEV, channels))
    return stacked.reshape(query_rows.shape)

def reference(tokens, norm_gain, query_weight, key_weight, value_weight, head_scale, out_weight, mlp_gain, up_weight, down_weight):
    channels = tokens.shape[-1]
    scaling = head_scale / math.sqrt(channels // HEADS)
    normed = layer_norm(tokens, norm_gain)
    queries = project(normed, query_weight)
    fine_out = level_attend(wrap_pad(project(normed, key_weight)), wrap_pad(project(normed, value_weight)), queries, scaling)
    middle = pooled_mean(normed, 2)
    middle_out = level_attend(wrap_pad(project(middle, key_weight)), wrap_pad(project(middle, value_weight)), queries, scaling)
    coarse = pooled_mean(normed, 4).reshape(-1, channels)
    coarse_out = coarse_attend(queries.reshape(-1, channels), project(coarse, key_weight), project(coarse, value_weight), scaling)
    attended = (fine_out + middle_out + coarse_out.reshape(tokens.shape)).astype(jnp.bfloat16)
    flat_tokens = tokens.reshape(-1, channels)
    residual = (flat_tokens.astype(jnp.float32) + jnp.dot(attended.reshape(-1, channels), out_weight, preferred_element_type=jnp.float32)).astype(jnp.bfloat16)
    second = layer_norm(residual, mlp_gain)
    hidden = jax.nn.gelu(jnp.dot(second, up_weight, preferred_element_type=jnp.float32), approximate=True).astype(jnp.bfloat16)
    output = residual.astype(jnp.float32) + jnp.dot(hidden, down_weight, preferred_element_type=jnp.float32)
    return output.astype(jnp.bfloat16).reshape(tokens.shape)
```

```python
import functools
import math

import jax
import jax.numpy as jnp
import numpy as np
from jax import lax
from jax.experimental import pallas as pl
from jax.experimental.pallas import tpu as pltpu
from jax.sharding import PartitionSpec as P

HEADS = 8
EPSILON = 1e-05
LOG2E = 1.4426950408889634
NEGATIVE = -1e30
LANES = 128
F32 = jnp.float32
BF16 = jnp.bfloat16
AXES = ("gx", "gy", "gz")


def up_to(count, step):
    return -(-count // step) * step


def in_vmem(array):
    return pltpu.with_memory_space_constraint(array, pltpu.VMEM)


def layer_norm(values, gain):
    average = jnp.mean(values, axis=-1, keepdims=True)
    centered = values - average
    variance = jnp.mean(centered * centered, axis=-1, keepdims=True)
    return (centered * lax.rsqrt(variance + EPSILON) * gain).astype(BF16)


def dot(left, right):
    return jnp.dot(left, right, preferred_element_type=F32)


def dot_nt(left, right):
    return lax.dot_general(left, right, (((1,), (1,)), ((), ())), preferred_element_type=F32)


def dot_tn(left, right):
    return lax.dot_general(left, right, (((0,), (0,)), ((), ())), preferred_element_type=F32)


def joined(ref, rows):
    return jnp.concatenate([ref[j, rows, :] for j in range(ref.shape[0])], axis=1)


def call(kernel, outs, *args, scratch=(), vmem=True, limit=24 << 20):
    kinds = [pltpu.VMEM(s, d) if vmem else jax.ShapeDtypeStruct(s, d) for s, d in outs]
    return pl.pallas_call(
        kernel,
        out_shape=kinds,
        in_specs=[
            pl.BlockSpec(memory_space=pltpu.SMEM)
            if a.dtype == jnp.int32
            else pl.BlockSpec(memory_space=pltpu.VMEM)
            for a in args
        ],
        out_specs=[pl.BlockSpec(memory_space=pltpu.VMEM) for _ in outs],
        scratch_shapes=list(scratch),
        compiler_params=pltpu.CompilerParams(vmem_limit_bytes=limit),
    )(*args)


class Sizes:
    def __init__(self, extent, channels):
        self.x, self.y, self.z = extent
        self.c = channels
        self.parts = channels // LANES
        self.cells = self.x * self.y * self.z
        self.mx, self.my, self.mz = (n // 2 for n in extent)
        self.mids = self.mx * self.my * self.mz
        self.coarse = self.mids // 8
        self.zp = up_to(self.z + 2, 16)
        self.mzp = up_to(self.mz + 2, 8)
        self.fine_rows = (self.x + 2) * (self.y + 2) * self.zp
        self.mid_rows = (self.mx + 2) * (self.my + 2) * self.mzp
        self.fx, self.gx = self.y * self.z, self.my * self.mz
        self.fy, self.gy = (self.x + 2) * self.z, (self.mx + 2) * self.mz
        self.fz, self.gz = (self.x + 2) * (self.y + 2), (self.mx + 2) * (self.my + 2)


def pooling(size):
    x, y, z = np.unravel_index(np.arange(size.cells), (size.x, size.y, size.z))
    middle = ((x // 2) * size.my + y // 2) * size.mz + z // 2
    coarse = ((x // 4) * (size.my // 2) + y // 4) * (size.mz // 2) + z // 4
    rows = np.zeros((size.mids + up_to(size.coarse, 16), size.cells), np.float32)
    rows[middle, np.arange(size.cells)] = 1.0
    rows[size.mids + coarse, np.arange(size.cells)] = 1.0
    return rows.astype(jnp.bfloat16)


def window_bias(length, padded, query_cells, factor, z_cells):
    place = np.arange(padded)
    key = np.where(place < length, place, np.where(place == length, -1, length))
    query_z = np.arange(query_cells) % z_cells
    start = 2 * (query_z // factor)
    seen = (key[:, None] >= start - 1) & (key[:, None] <= start + 2) & (place[:, None] < length + 2)
    bias = np.where(seen, 0.0, NEGATIVE).astype(np.float32)
    return np.tile(bias, (1, HEADS))


def first_kernel(size, odd, tokens, gain, pool, normed, middle, face_a, face_b, coarse_out):
    values = layer_norm(tokens[...].astype(F32), gain[...])
    normed[...] = values
    pooled = dot(pool[...], values)
    mids = (pooled[: size.mids] * 0.125).astype(BF16)
    middle[...] = mids
    coarse_out[...] = (pooled[size.mids :] * (1.0 / 64.0)).astype(BF16)
    high = jnp.concatenate([values[size.cells - size.fx :], mids[size.mids - size.gx :]], axis=0)
    low = jnp.concatenate([values[: size.fx], mids[: size.gx]], axis=0)
    is_odd = odd[0] == 1
    face_a[...] = jnp.where(is_odd, low, high)
    face_b[...] = jnp.where(is_odd, high, low)


def pick(odd, from_a, from_b):
    is_odd = odd == 1
    first, second = from_a[...].astype(F32), from_b[...].astype(F32)
    return jnp.where(is_odd, first, second), jnp.where(is_odd, second, first)


def y_kernel(size, odd, normed, middle, from_a, from_b, face):
    low, high = pick(odd[0], from_a, from_b)
    cells = normed[...].astype(F32).reshape(size.x, size.y, size.z, size.c)
    mids = middle[...].astype(F32).reshape(size.mx, size.my, size.mz, size.c)
    parts = []
    for at, mat in ((0, 0), (size.y - 1, size.my - 1)):
        fine_low = low[: size.fx].reshape(size.y, size.z, size.c)[at]
        fine_high = high[: size.fx].reshape(size.y, size.z, size.c)[at]
        mid_low = low[size.fx :].reshape(size.my, size.mz, size.c)[mat]
        mid_high = high[size.fx :].reshape(size.my, size.mz, size.c)[mat]
        own = cells[:, at].reshape(size.x * size.z, size.c)
        own_mid = mids[:, mat].reshape(size.mx * size.mz, size.c)
        parts.append(
            jnp.concatenate([fine_low, own, fine_high, mid_low, own_mid, mid_high], axis=0)
        )
    face[...] = jnp.concatenate(parts, axis=0).astype(BF16)


def fill(size, odd_x, normed, middle, from_a, from_b, y_low, y_high, fine, mid):
    low, high = pick(odd_x, from_a, from_b)
    fine[...] = jnp.zeros_like(fine)
    mid[...] = jnp.zeros_like(mid)
    cells = normed[...].astype(F32)
    mids = middle[...].astype(F32)

    def put(x, y, run):
        at = (x * (size.y + 2) + y) * size.zp
        for j in range(size.parts):
            fine[j, at : at + size.z, :] = run[:, j * LANES : (j + 1) * LANES]

    def put_mid(x, y, run):
        at = (x * (size.my + 2) + y) * size.mzp
        for j in range(size.parts):
            mid[j, at : at + size.mz, :] = run[:, j * LANES : (j + 1) * LANES]

    for x in range(size.x):
        for y in range(size.y):
            at = (x * size.y + y) * size.z
            put(x + 1, y + 1, cells[at : at + size.z])
    for x in range(size.mx):
        for y in range(size.my):
            at = (x * size.my + y) * size.mz
            put_mid(x + 1, y + 1, mids[at : at + size.mz])
    for x, halo in ((0, low), (size.x + 1, high)):
        for y in range(size.y):
            put(x, y + 1, halo[y * size.z : (y + 1) * size.z])
    for x, halo in ((0, low), (size.mx + 1, high)):
        for y in range(size.my):
            put_mid(x, y + 1, halo[size.fx + y * size.mz : size.fx + (y + 1) * size.mz])
    for y, my, halo in ((0, 0, y_low), (size.y + 1, size.my + 1, y_high)):
        for x in range(size.x + 2):
            put(x, y, halo[x * size.z : (x + 1) * size.z])
        for x in range(size.mx + 2):
            put_mid(x, my, halo[size.fy + x * size.mz : size.fy + (x + 1) * size.mz])


def z_kernel(size, pair, odd, normed, middle, from_a, from_b, *refs):
    y_refs, (face_a, face_b, fine, mid) = refs[: 1 if pair else 2], refs[1 if pair else 2 :]
    half = size.fy + size.gy
    if pair:
        both = y_refs[0][...].astype(F32)
        y_low, y_high = both[half:], both[:half]
    else:
        y_low = y_refs[0][...].astype(F32)
        y_high = y_refs[1][...].astype(F32)
    fill(size, odd[0], normed, middle, from_a, from_b, y_low, y_high, fine, mid)

    def cut(z, mz):
        return jnp.concatenate(
            [
                joined(fine, pl.ds(z, size.fz, stride=size.zp)),
                joined(mid, pl.ds(mz, size.gz, stride=size.mzp)),
            ],
            axis=0,
        )

    low, high = cut(0, 0), cut(size.z - 1, size.mz - 1)
    is_odd = odd[1] == 1
    face_a[...] = jnp.where(is_odd, low, high).astype(BF16)
    face_b[...] = jnp.where(is_odd, high, low).astype(BF16)


def last_kernel(
    size,
    coarse_rows,
    n_coarse,
    odd,
    scale,
    tokens,
    fine,
    mid,
    from_a,
    from_b,
    query_weight,
    key_weight,
    value_weight,
    out_weight,
    mlp_gain,
    up_weight,
    down_weight,
    fine_bias,
    mid_bias,
    mask,
    *refs,
):
    coarse_refs, (out, fine_pad, mid_pad, keys, values, queries, attended) = refs[:n_coarse], refs[n_coarse:]
    low, high = pick(odd[1], from_a, from_b)
    fine_pad[...] = fine[...]
    mid_pad[...] = mid[...]
    for j in range(size.parts):
        lanes = slice(j * LANES, (j + 1) * LANES)
        fine_pad[j, pl.ds(size.z, size.fz, stride=size.zp), :] = low[: size.fz, lanes]
        fine_pad[j, pl.ds(size.z + 1, size.fz, stride=size.zp), :] = high[: size.fz, lanes]
        mid_pad[j, pl.ds(size.mz, size.gz, stride=size.mzp), :] = low[size.fz :, lanes]
        mid_pad[j, pl.ds(size.mz + 1, size.gz, stride=size.mzp), :] = high[size.fz :, lanes]

    whole = joined(fine_pad, slice(None))
    sources = [whole.astype(BF16), joined(mid_pad, slice(None)).astype(BF16)]
    sources.append(jnp.concatenate([r[...] for r in coarse_refs], axis=0))
    cells = jnp.concatenate(sources, axis=0)
    keys[...] = dot(cells, key_weight[...]).astype(BF16)
    values[...] = dot(cells, value_weight[...]).astype(BF16)
    own = whole.reshape(size.x + 2, size.y + 2, size.zp, size.c)
    own = own[1 : size.x + 1, 1 : size.y + 1, : size.z].reshape(size.cells, size.c)
    queries[...] = dot(own.astype(BF16), query_weight[...]).astype(BF16)

    mid_at = size.fine_rows
    coarse_at = mid_at + size.mid_rows
    run = 2 * size.z
    group = 2 * run
    fine_row = (size.y + 2) * size.zp
    mid_row = (size.my + 2) * size.mzp

    def weigh(scores, bias, length):
        scores = scores * scale[...]
        if bias is not None:
            scores = (scores.reshape(-1, length, scores.shape[-1]) + bias[...][None]).reshape(scores.shape)
        weights = jnp.exp2(scores - jnp.max(scores, axis=0, keepdims=True))
        return (weights * (1.0 / jnp.sum(weights, axis=0, keepdims=True))).astype(BF16)

    groups_y = size.y // 2

    def one_group(index, carry):
        bx, by = index // groups_y, index % groups_y
        rows = [
            pl.ds(pl.multiple_of(((2 * bx + dx) * size.y + 2 * by) * size.z, 16), run) for dx in (0, 1)
        ]
        some = jnp.concatenate([queries[r, :] for r in rows], axis=0)
        spread = jnp.concatenate([some] * HEADS, axis=0) * mask[...]
        fine_slabs = [
            pl.ds(pl.multiple_of((2 * bx + k) * fine_row + 2 * by * size.zp, 16), 4 * size.zp)
            for k in range(4)
        ]
        mid_slabs = [
            pl.ds(
                pl.multiple_of(
                    mid_at + (2 * (bx // 2) + k) * mid_row + 2 * (by // 2) * size.mzp, 16
                ),
                4 * size.mzp,
            )
            for k in range(4)
        ]
        coarse_slabs = [pl.ds(coarse_at, coarse_rows)]
        total = None
        for slabs, bias, length in (
            (fine_slabs, fine_bias, size.zp),
            (mid_slabs, mid_bias, size.mzp),
            (coarse_slabs, None, 0),
        ):
            some_keys = jnp.concatenate([keys[s, :] for s in slabs], axis=0)
            some_values = jnp.concatenate([values[s, :] for s in slabs], axis=0)
            weights = weigh(dot_nt(some_keys, spread), bias, length)
            part = dot_tn(weights, some_values)
            total = part if total is None else total + part
        total = total.reshape(HEADS, group, size.c)
        wide = mask[...].astype(F32).reshape(HEADS, group, size.c)
        result = jnp.sum(total * wide, axis=0).astype(BF16)
        for k, r in enumerate(rows):
            attended[r, :] = result[k * run : (k + 1) * run]
        return carry

    lax.fori_loop(0, (size.x // 2) * groups_y, one_group, 0, unroll=True)
    residual = (tokens[...].astype(F32) + dot(attended[...], out_weight[...])).astype(BF16)
    second = layer_norm(residual.astype(F32), mlp_gain[...])
    hidden = jax.nn.gelu(dot(second, up_weight[...]), approximate=True).astype(BF16)
    out[...] = (residual.astype(F32) + dot(hidden, down_weight[...])).astype(BF16)


def swap(array, axis, start):
    count = lax.axis_size(axis)
    pairs = []
    for i in range(start, count, 2):
        other = (i + 1) % count
        pairs += [(i, other), (other, i)]
    return lax.ppermute(array, axis, pairs)


def shift(array, axis, by):
    count = lax.axis_size(axis)
    return lax.ppermute(array, axis, [(i, (i + by) % count) for i in range(count)])


def shards(
    tokens,
    norm_gain,
    query_weight,
    key_weight,
    value_weight,
    head_scale,
    out_weight,
    mlp_gain,
    up_weight,
    down_weight,
):
    channels = tokens.shape[-1]
    size = Sizes(tokens.shape[:3], channels)
    nx, ny, nz = (lax.axis_size(a) for a in AXES)
    flat = tokens.reshape(size.cells, channels)
    odd = jnp.stack([lax.axis_index("gx") % 2, lax.axis_index("gz") % 2]).astype(jnp.int32)
    coarse_rows = up_to(size.coarse, 16)

    fx, gx, fy, gy, fz, gz = size.fx, size.gx, size.fy, size.gy, size.fz, size.gz
    normed, middle, face_a, face_b, coarse = call(
        functools.partial(first_kernel, size),
        [
            ((size.cells, channels), BF16),
            ((size.mids, channels), BF16),
            ((fx + gx, channels), BF16),
            ((fx + gx, channels), BF16),
            ((coarse_rows, channels), BF16),
        ],
        odd,
        flat,
        norm_gain.reshape(1, -1),
        jnp.asarray(pooling(size)),
    )
    from_a = in_vmem(swap(face_a, "gx", 0))
    from_b = in_vmem(swap(face_b, "gx", 1))
    faces = call(
        functools.partial(y_kernel, size),
        [((2 * (fy + gy), channels), BF16)],
        odd,
        normed,
        middle,
        from_a,
        from_b,
    )[0]
    if ny == 2:
        from_y = [in_vmem(swap(faces, "gy", 0))]
    else:
        from_y = [
            in_vmem(shift(faces[fy + gy :], "gy", 1)),
            in_vmem(shift(faces[: fy + gy], "gy", -1)),
        ]
    z_a, z_b, fine, mid = call(
        functools.partial(z_kernel, size, ny == 2),
        [
            ((fz + gz, channels), BF16),
            ((fz + gz, channels), BF16),
            ((size.parts, size.fine_rows, LANES), F32),
            ((size.parts, size.mid_rows, LANES), F32),
        ],
        odd,
        normed,
        middle,
        from_a,
        from_b,
        *from_y,
    )
    got_a = in_vmem(swap(z_a, "gz", 0))
    got_b = in_vmem(swap(z_b, "gz", 1))
    gathered = lax.all_to_all(
        jnp.broadcast_to(coarse[None, : size.coarse], (nx * ny * nz, size.coarse, channels)), AXES, 0, 0
    ).reshape(-1, channels)

    total_coarse = gathered.shape[0]
    key_rows = size.fine_rows + size.mid_rows + total_coarse
    group = 4 * size.z
    head = np.arange(HEADS * group) // group
    mask = (head[:, None] == np.arange(channels)[None, :] // (channels // HEADS)).astype(jnp.bfloat16)
    scale = jnp.repeat(head_scale * (LOG2E / math.sqrt(channels // HEADS)), group).reshape(1, -1)
    out = call(
        functools.partial(last_kernel, size, total_coarse, 1),
        [((size.cells, channels), BF16)],
        odd,
        scale,
        flat,
        fine,
        mid,
        got_a,
        got_b,
        query_weight,
        key_weight,
        value_weight,
        out_weight,
        mlp_gain.reshape(1, -1),
        up_weight,
        down_weight,
        jnp.asarray(window_bias(size.z, size.zp, group, 2, size.z)),
        jnp.asarray(window_bias(size.mz, size.mzp, group, 4, size.z)),
        jnp.asarray(mask),
        gathered,
        scratch=[
            pltpu.VMEM((size.parts, size.fine_rows, LANES), F32),
            pltpu.VMEM((size.parts, size.mid_rows, LANES), F32),
            pltpu.VMEM((key_rows, channels), BF16),
            pltpu.VMEM((key_rows, channels), BF16),
            pltpu.VMEM((size.cells, channels), BF16),
            pltpu.VMEM((size.cells, channels), BF16),
        ],
        vmem=False,
    )[0]
    return out.reshape(tokens.shape)


def solution(mesh):
    in_specs = (P("gx", "gy", "gz", None), P(), P(), P(), P(), P(), P(), P(), P(), P())
    out_specs = P("gx", "gy", "gz", None)
    return jax.shard_map(shards, mesh=mesh, in_specs=in_specs, out_specs=out_specs, check_vma=False)
```

```python
import functools
import math

import jax
import jax.numpy as jnp
import numpy as np
from jax import lax
from jax.experimental import pallas as pl
from jax.experimental.pallas import tpu as pltpu
from jax.sharding import PartitionSpec as P

HEADS = 8
EPSILON = 1e-05
LOG2E = 1.4426950408889634
NEGATIVE = -1e30
LANES = 128
F32 = jnp.float32
BF16 = jnp.bfloat16
AXES = ("gx", "gy", "gz")


def up_to(count, step):
    return -(-count // step) * step


def layer_norm(values, gain):
    average = jnp.mean(values, axis=-1, keepdims=True)
    centered = values - average
    variance = jnp.mean(centered * centered, axis=-1, keepdims=True)
    return (centered * lax.rsqrt(variance + EPSILON) * gain).astype(BF16)


def dot(left, right):
    return jnp.dot(left, right, preferred_element_type=F32)


def dot_nt(left, right):
    return lax.dot_general(left, right, (((1,), (1,)), ((), ())), preferred_element_type=F32)


def dot_tn(left, right):
    return lax.dot_general(left, right, (((0,), (0,)), ((), ())), preferred_element_type=F32)


def joined(ref, rows):
    return jnp.concatenate([ref[j, rows, :] for j in range(ref.shape[0])], axis=1)


def split_store(ref, rows, values):
    for j in range(ref.shape[0]):
        ref[j, rows, :] = values[:, j * LANES : (j + 1) * LANES]


def call(kernel, outs, *args, spaces=None, scratch=(), vmem=True, aliases=None, limit=24 << 20, work=None):
    kinds = [pltpu.VMEM(s, d) if vmem else jax.ShapeDtypeStruct(s, d) for s, d in outs]
    spaces = spaces or [pltpu.VMEM] * len(args)
    return pl.pallas_call(
        kernel,
        out_shape=kinds,
        in_specs=[pl.BlockSpec(memory_space=s) for s in spaces],
        out_specs=[pl.BlockSpec(memory_space=pltpu.VMEM) for _ in outs],
        scratch_shapes=list(scratch),
        input_output_aliases=aliases or {},
        compiler_params=pltpu.CompilerParams(vmem_limit_bytes=limit),
        cost_estimate=work and pl.CostEstimate(flops=work, bytes_accessed=0, transcendentals=0),
    )(*args)


class Sizes:
    def __init__(self, extent, channels):
        self.x, self.y, self.z = extent
        self.c = channels
        self.parts = channels // LANES
        self.cells = self.x * self.y * self.z
        self.mx, self.my, self.mz = (n // 2 for n in extent)
        self.mids = self.mx * self.my * self.mz
        self.coarse = self.mids // 8
        self.mzp = up_to(self.mz + 2, 8)
        self.fine_rows = (self.x + 2) * (self.y + 2) * self.z
        self.mid_rows = (self.mx + 2) * (self.my + 2) * self.mzp
        self.fy, self.gy = self.x * self.z, self.mx * self.mz
        self.fx, self.gx = (self.y + 2) * self.z, (self.my + 2) * self.mz
        self.fz, self.gz = (self.x + 2) * (self.y + 2), (self.mx + 2) * (self.my + 2)
        self.fzp, self.gzp = up_to(self.fz, 8), up_to(self.gz, 8)
        self.groups = [(bx, by) for bx in range(self.x // 2) for by in range(self.y // 2)]
        self.group = 4 * self.z

    def query_rows(self, bx, by):
        return [
            slice(((2 * bx + dx) * self.y + 2 * by) * self.z, ((2 * bx + dx) * self.y + 2 * by + 2) * self.z)
            for dx in (0, 1)
        ]


def pooling(size):
    x, y, z = np.unravel_index(np.arange(size.cells), (size.x, size.y, size.z))
    middle = ((x // 2) * size.my + y // 2) * size.mz + z // 2
    coarse = ((x // 4) * (size.my // 2) + y // 4) * (size.mz // 2) + z // 4
    rows = np.zeros((size.mids + size.coarse, size.cells), np.float32)
    rows[middle, np.arange(size.cells)] = 1.0
    rows[size.mids + coarse, np.arange(size.cells)] = 1.0
    grid = rows[: size.mids].reshape(size.mx, size.my, size.mz, size.cells)
    faces = [grid[:, at].reshape(size.gy, size.cells) for at in (0, size.my - 1)]
    return np.concatenate([rows, rows[size.mids :], *faces]).astype(jnp.bfloat16)


def window_bias(size):
    query_z = np.arange(size.group) % size.z

    def seen(keys, factor):
        start = 2 * (query_z // factor)
        return (keys[:, None] >= start - 1) & (keys[:, None] <= start + 2)

    place = np.arange(size.mzp)
    middle = np.where(place < size.mz, place, np.where(place == size.mz, -1, size.mz))
    held = seen(middle, 4) & (place[:, None] < size.mz + 2)
    rows = np.concatenate([seen(np.arange(size.z), 2), held, seen(np.array([-1, size.z]), 2)])
    bias = np.where(rows, 0.0, NEGATIVE).astype(np.float32)
    bias = np.concatenate([bias, np.zeros((up_to(len(bias), 8) - len(bias), size.group), np.float32)])
    return np.tile(bias, (1, HEADS))


def arranging(size):
    rows = np.zeros((len(size.groups) * 32, 2 * size.fzp), np.float32)
    at = 0
    for bx, by in size.groups:
        for side in range(2):
            for kx in range(4):
                for ky in range(4):
                    rows[at, side * size.fzp + (2 * bx + kx) * (size.y + 2) + 2 * by + ky] = 1.0
                    at += 1
    return rows.astype(jnp.bfloat16)


def head_mask(size):
    head = np.arange(HEADS * size.group) // size.group
    return (head[:, None] == np.arange(size.c)[None, :] // (size.c // HEADS)).astype(jnp.bfloat16)


def fetch(sources, targets, sems):
    copies = [pltpu.make_async_copy(s, t, sems.at[i]) for i, (s, t) in enumerate(zip(sources, targets))]
    for copy in copies:
        copy.start()
    return copies


def is_odd(axis):
    return lax.axis_index(axis) % 2 == 1


def first_kernel(size, devices, tokens, gain, pool, both, faces, coarse_out, cells, gain_here, pool_here, sems):
    copies = fetch((tokens, gain, pool), (cells, gain_here, pool_here), sems)
    for copy in copies[:2]:
        copy.wait()
    values = layer_norm(cells[...].astype(F32), gain_here[...])
    both[: size.cells, :] = values
    copies[2].wait()
    pooled = dot(pool_here[...], values)
    at = size.mids + 2 * size.coarse
    both[size.cells :, :] = (pooled[: size.mids] * 0.125).astype(BF16)
    pack = (pooled[size.mids : at] * (1.0 / 64.0)).astype(BF16)
    for row in range(0, devices * size.coarse, 2 * size.coarse):
        coarse_out[row : row + 2 * size.coarse, :] = pack
    face = size.fy + size.gy
    for side, y in enumerate((0, size.y - 1)):
        rows = [slice((x * size.y + y) * size.z, (x * size.y + y + 1) * size.z) for x in range(size.x)]
        cut = jnp.concatenate([values[r].astype(F32) for r in rows], axis=0)
        faces[side * face : side * face + size.fy, :] = cut.astype(BF16)
        mids = pooled[at + side * size.gy : at + (side + 1) * size.gy] * 0.125
        faces[side * face + size.fy : (side + 1) * face, :] = mids.astype(BF16)


def prepare_kernel(size, both, after, *refs):
    held = (len(refs) - 4) // 2
    sources, targets = refs[:held], refs[held : 2 * held]
    queries, fine, mid, sems = refs[2 * held :]
    copies = fetch(sources, targets, sems)
    cells = both[: size.cells, :].astype(F32)
    mids = both[size.cells :, :].astype(F32)
    mid[...] = jnp.zeros_like(mid)
    for x in range(size.x):
        at = ((x + 1) * (size.y + 2) + 1) * size.z
        split_store(fine, slice(at, at + size.y * size.z), cells[x * size.y * size.z : (x + 1) * size.y * size.z])
    for x in range(size.mx):
        for y in range(size.my):
            at = ((x + 1) * (size.my + 2) + y + 1) * size.mzp
            row = (x * size.my + y) * size.mz
            split_store(mid, slice(at, at + size.mz), mids[row : row + size.mz])
    copies[0].wait()
    queries[...] = dot(both[: size.cells, :], targets[0][...]).astype(BF16)
    for copy in copies[1:]:
        copy.wait()


def pick(odd, from_a, from_b):
    first, second = from_a[...].astype(F32), from_b[...].astype(F32)
    return jnp.where(odd, first, second), jnp.where(odd, second, first)


def from_sides(size, y_refs):
    if len(y_refs) == 1:
        both = y_refs[0][...].astype(F32)
        return both[size.fy + size.gy :], both[: size.fy + size.gy]
    return y_refs[0][...].astype(F32), y_refs[1][...].astype(F32)


def x_kernel(size, both, *refs):
    y_refs, (face_a, face_b) = refs[:-2], refs[-2:]
    y_low, y_high = from_sides(size, y_refs)
    cells = both[: size.cells, :].astype(F32)
    mids = both[size.cells :, :].astype(F32)

    def cut(x, mx):
        fine_at, own = slice(x * size.z, (x + 1) * size.z), size.y * size.z
        mid_at, own_mid = slice(size.fy + mx * size.mz, size.fy + (mx + 1) * size.mz), size.my * size.mz
        return jnp.concatenate(
            [
                y_low[fine_at],
                cells[x * own : (x + 1) * own],
                y_high[fine_at],
                y_low[mid_at],
                mids[mx * own_mid : (mx + 1) * own_mid],
                y_high[mid_at],
            ],
            axis=0,
        )

    low, high = cut(0, 0), cut(size.x - 1, size.mx - 1)
    odd = is_odd("gx")
    face_a[...] = jnp.where(odd, low, high).astype(BF16)
    face_b[...] = jnp.where(odd, high, low).astype(BF16)


def z_kernel(size, fine_in, mid_in, from_a, from_b, *refs):
    y_refs, (face_a, face_b, fine, mid) = refs[:-4], refs[-4:]
    y_low, y_high = from_sides(size, y_refs)
    low, high = pick(is_odd("gx"), from_a, from_b)
    for x, halo in ((0, low), (size.x + 1, high)):
        split_store(fine, slice(x * size.fx, (x + 1) * size.fx), halo[: size.fx])
    for x, halo in ((0, low), (size.mx + 1, high)):
        for y in range(size.my + 2):
            at = (x * (size.my + 2) + y) * size.mzp
            row = size.fx + y * size.mz
            split_store(mid, slice(at, at + size.mz), halo[row : row + size.mz])
    for y, my, halo in ((0, 0, y_low), (size.y + 1, size.my + 1, y_high)):
        for x in range(size.x):
            at = ((x + 1) * (size.y + 2) + y) * size.z
            split_store(fine, slice(at, at + size.z), halo[x * size.z : (x + 1) * size.z])
        for x in range(size.mx):
            at = ((x + 1) * (size.my + 2) + my) * size.mzp
            row = size.fy + x * size.mz
            split_store(mid, slice(at, at + size.mz), halo[row : row + size.mz])

    def cut(z, mz):
        parts = [
            joined(fine, pl.ds(z, size.fz, stride=size.z)),
            jnp.zeros((size.fzp - size.fz, size.c), F32),
            joined(mid, pl.ds(mz, size.gz, stride=size.mzp)),
            jnp.zeros((size.gzp - size.gz, size.c), F32),
        ]
        return jnp.concatenate([p for p in parts if p.shape[0]], axis=0)

    below, above = cut(0, 0), cut(size.z - 1, size.mz - 1)
    odd = is_odd("gz")
    face_a[...] = jnp.where(odd, below, above).astype(BF16)
    face_b[...] = jnp.where(odd, above, below).astype(BF16)


def lane_scale(size, head_scale):
    factor = LOG2E / math.sqrt(size.c // HEADS)
    return jnp.concatenate([jnp.full((1, size.group), head_scale[h] * factor, F32) for h in range(HEADS)], axis=1)


def spread_queries(size, queries, rows, mask):
    some = jnp.concatenate([queries[r, :] for r in rows], axis=0)
    return jnp.concatenate([some] * HEADS, axis=0) * mask


def soft(scores):
    weights = jnp.exp2(scores - jnp.max(scores, axis=0, keepdims=True))
    return (weights * (1.0 / jnp.sum(weights, axis=0, keepdims=True))).astype(BF16)


def gather_heads(size, total, wide):
    return jnp.sum(total.reshape(HEADS, size.group, size.c) * wide, axis=0)


def coarse_kernel(
    size, head_scale, queries, fine, coarse, key_weight, value_weight, mask, coarse_out, keys, values, scale_here, sems
):
    copy = fetch((head_scale,), (scale_here,), sems)[0]
    block = joined(fine, slice(None)).astype(BF16)
    keys[...] = dot(block, key_weight[...]).astype(BF16)
    values[...] = dot(block, value_weight[...]).astype(BF16)
    cells = coarse[...]
    coarse_keys = dot(cells, key_weight[...]).astype(BF16)
    coarse_values = dot(cells, value_weight[...]).astype(BF16)
    copy.wait()
    scale = lane_scale(size, scale_here)
    spread_mask = mask[...]
    wide = spread_mask.astype(F32).reshape(HEADS, size.group, size.c)
    for bx, by in size.groups:
        rows = size.query_rows(bx, by)
        spread = spread_queries(size, queries, rows, spread_mask)
        total = dot_tn(soft(dot_nt(coarse_keys, spread) * scale), coarse_values)
        result = gather_heads(size, total, wide)
        for k, r in enumerate(rows):
            coarse_out[r, :] = result[k * 2 * size.z : (k + 1) * 2 * size.z]


def last_kernel(
    size,
    head_scale,
    tokens,
    mlp_gain,
    biases,
    queries,
    keys,
    values,
    mid_in,
    from_a,
    from_b,
    coarse_out,
    key_weight,
    value_weight,
    out_weight,
    up_weight,
    down_weight,
    mask,
    arrange,
    out,
    mid,
    attended,
    scale_here,
    tokens_here,
    gain_here,
    bias,
    sems,
):
    copies = fetch((biases, head_scale, tokens, mlp_gain), (bias, scale_here, tokens_here, gain_here), sems)
    low, high = pick(is_odd("gz"), from_a, from_b)
    mid[...] = mid_in[...]
    split_store(mid, pl.ds(size.mz, size.gz, stride=size.mzp), low[size.fzp : size.fzp + size.gz])
    split_store(mid, pl.ds(size.mz + 1, size.gz, stride=size.mzp), high[size.fzp : size.fzp + size.gz])
    ends = jnp.concatenate([low[: size.fzp], high[: size.fzp]], axis=0).astype(BF16)
    ends = dot(arrange[...], ends).astype(BF16)
    end_keys = dot(ends, key_weight[...]).astype(BF16)
    end_values = dot(ends, value_weight[...]).astype(BF16)
    mids = joined(mid, slice(None)).astype(BF16)
    mid_keys = dot(mids, key_weight[...]).astype(BF16)
    mid_values = dot(mids, value_weight[...]).astype(BF16)

    for copy in copies:
        copy.wait()
    scale = lane_scale(size, scale_here)
    spread_mask = mask[...]
    wide = spread_mask.astype(F32).reshape(HEADS, size.group, size.c)
    run_bias = bias[: size.z]
    mid_bias = bias[size.z : size.z + size.mzp]
    low_bias = bias[size.z + size.mzp : size.z + size.mzp + 1]
    high_bias = bias[size.z + size.mzp + 1 : size.z + size.mzp + 2]
    fine_row = (size.y + 2) * size.z
    mid_row = (size.my + 2) * size.mzp

    def tiled(scores, one):
        length = one.shape[0]
        return (scores.reshape(-1, length, scores.shape[-1]) + one[None]).reshape(scores.shape)

    for index, (bx, by) in enumerate(size.groups):
        rows = size.query_rows(bx, by)
        spread = spread_queries(size, queries, rows, spread_mask)
        slabs = [
            slice((2 * bx + k) * fine_row + 2 * by * size.z, (2 * bx + k) * fine_row + (2 * by + 4) * size.z)
            for k in range(4)
        ]
        ends_at = slice(32 * index, 32 * index + 32)
        some_keys = jnp.concatenate([keys[s, :] for s in slabs] + [end_keys[ends_at]], axis=0)
        some_values = jnp.concatenate([values[s, :] for s in slabs] + [end_values[ends_at]], axis=0)
        scores = dot_nt(some_keys, spread) * scale
        inner = 16 * size.z
        scores = jnp.concatenate(
            [
                tiled(scores[:inner], run_bias),
                scores[inner : inner + 16] + low_bias,
                scores[inner + 16 :] + high_bias,
            ],
            axis=0,
        )
        total = dot_tn(soft(scores), some_values)
        slabs = [
            slice(
                (2 * (bx // 2) + k) * mid_row + 2 * (by // 2) * size.mzp,
                (2 * (bx // 2) + k) * mid_row + (2 * (by // 2) + 4) * size.mzp,
            )
            for k in range(4)
        ]
        some_keys = jnp.concatenate([mid_keys[s] for s in slabs], axis=0)
        some_values = jnp.concatenate([mid_values[s] for s in slabs], axis=0)
        scores = tiled(dot_nt(some_keys, spread) * scale, mid_bias)
        total = total + dot_tn(soft(scores), some_values)
        result = gather_heads(size, total, wide)
        for k, r in enumerate(rows):
            part = result[k * 2 * size.z : (k + 1) * 2 * size.z]
            attended[r, :] = (part + coarse_out[r, :]).astype(BF16)

    residual = (tokens_here[...].astype(F32) + dot(attended[...], out_weight[...])).astype(BF16)
    second = layer_norm(residual.astype(F32), gain_here[...])
    hidden = jax.nn.gelu(dot(second, up_weight[...]), approximate=True).astype(BF16)
    out[...] = (residual.astype(F32) + dot(hidden, down_weight[...])).astype(BF16)


def swap(array, axis, start):
    count = lax.axis_size(axis)
    pairs = []
    for i in range(start, count, 2):
        other = (i + 1) % count
        pairs += [(i, other), (other, i)]
    return lax.ppermute(array, axis, pairs)


def shift(array, axis, by):
    count = lax.axis_size(axis)
    return lax.ppermute(array, axis, [(i, (i + by) % count) for i in range(count)])


def shards(
    tokens,
    norm_gain,
    query_weight,
    key_weight,
    value_weight,
    head_scale,
    out_weight,
    mlp_gain,
    up_weight,
    down_weight,
):
    channels = tokens.shape[-1]
    size = Sizes(tokens.shape[:3], channels)
    devices = math.prod(lax.axis_size(a) for a in AXES)
    fx, gx, fy, gy = size.fx, size.gx, size.fy, size.gy
    face_z = size.fzp + size.gzp
    smem, vmem, hbm = pltpu.SMEM, pltpu.VMEM, pltpu.HBM

    def pinned(*arrays):
        return [pltpu.with_memory_space_constraint(jnp.asarray(a), hbm) for a in arrays]

    flat, gain, gain_mlp, scales = pinned(
        tokens.reshape(size.cells, channels), norm_gain.reshape(1, -1), mlp_gain.reshape(1, -1), head_scale
    )
    biases, pool = pinned(window_bias(size), pooling(size))
    both, faces, coarse = call(
        functools.partial(first_kernel, size, devices),
        [
            ((size.cells + size.mids, channels), BF16),
            ((2 * (fy + gy), channels), BF16),
            ((devices * size.coarse, channels), BF16),
        ],
        flat,
        gain,
        pool,
        spaces=[hbm] * 3,
        scratch=[
            pltpu.VMEM(flat.shape, BF16),
            pltpu.VMEM(gain.shape, F32),
            pltpu.VMEM(pool.shape, BF16),
            pltpu.SemaphoreType.DMA((3,)),
        ],
    )
    if lax.axis_size("gy") == 2:
        from_y = [swap(faces, "gy", 0)]
    else:
        from_y = [shift(faces[fy + gy :], "gy", 1), shift(faces[: fy + gy], "gy", -1)]
    gathered = lax.all_to_all(coarse.reshape(devices, size.coarse, channels), AXES, 0, 0).reshape(-1, channels)
    face_a, face_b = call(
        functools.partial(x_kernel, size),
        [((fx + gx, channels), BF16), ((fx + gx, channels), BF16)],
        both,
        *from_y,
        work=20_000_000_000,
    )
    from_a = swap(face_a, "gx", 0)
    from_b = swap(face_b, "gx", 1)
    held = pinned(
        query_weight,
        key_weight,
        value_weight,
        head_mask(size),
        arranging(size),
        out_weight,
        up_weight,
        down_weight,
    )
    *weights, queries, fine, mid = call(
        functools.partial(prepare_kernel, size),
        [(a.shape, a.dtype) for a in held]
        + [
            ((size.cells, channels), BF16),
            ((size.parts, size.fine_rows, LANES), F32),
            ((size.parts, size.mid_rows, LANES), F32),
        ],
        both,
        face_a,
        *held,
        spaces=[vmem] * 2 + [hbm] * len(held),
        scratch=[pltpu.SemaphoreType.DMA((len(held),))],
    )
    wq, wk, wv, mask, arrange, wo, wu, wd = weights
    z_a, z_b, fine, mid = call(
        functools.partial(z_kernel, size),
        [
            ((face_z, channels), BF16),
            ((face_z, channels), BF16),
            ((size.parts, size.fine_rows, LANES), F32),
            ((size.parts, size.mid_rows, LANES), F32),
        ],
        fine,
        mid,
        from_a,
        from_b,
        *from_y,
        aliases={0: 2, 1: 3},
    )
    got_a = swap(z_a, "gz", 0)
    got_b = swap(z_b, "gz", 1)
    coarse_out, keys, values = call(
        functools.partial(coarse_kernel, size),
        [
            ((size.cells, channels), F32),
            ((size.fine_rows, channels), BF16),
            ((size.fine_rows, channels), BF16),
        ],
        scales,
        queries,
        fine,
        gathered,
        wk,
        wv,
        mask,
        spaces=[hbm] + [vmem] * 6,
        scratch=[pltpu.SMEM((HEADS,), F32), pltpu.SemaphoreType.DMA((1,))],
    )
    out = call(
        functools.partial(last_kernel, size),
        [((size.cells, channels), BF16)],
        scales,
        flat,
        gain_mlp,
        biases,
        queries,
        keys,
        values,
        mid,
        got_a,
        got_b,
        coarse_out,
        wk,
        wv,
        wo,
        wu,
        wd,
        mask,
        arrange,
        spaces=[hbm] * 4 + [vmem] * 14,
        scratch=[
            pltpu.VMEM((size.parts, size.mid_rows, LANES), F32),
            pltpu.VMEM((size.cells, channels), BF16),
            pltpu.SMEM((HEADS,), F32),
            pltpu.VMEM(flat.shape, BF16),
            pltpu.VMEM(gain_mlp.shape, F32),
            pltpu.VMEM(biases.shape, F32),
            pltpu.SemaphoreType.DMA((4,)),
        ],
        vmem=False,
    )[0]
    return out.reshape(tokens.shape)


def solution(mesh):
    in_specs = (P("gx", "gy", "gz", None), P(), P(), P(), P(), P(), P(), P(), P(), P())
    out_specs = P("gx", "gy", "gz", None)
    return jax.shard_map(shards, mesh=mesh, in_specs=in_specs, out_specs=out_specs, check_vma=False)
```

```python
import functools
import math

import jax
import jax.numpy as jnp
import numpy as np
from jax import lax
from jax.experimental import pallas as pl
from jax.experimental.pallas import tpu as pltpu
from jax.sharding import PartitionSpec as P

HEADS = 8
EPSILON = 1e-05
LOG2E = 1.4426950408889634
NEGATIVE = -1e30
LANES = 128
F32 = jnp.float32
BF16 = jnp.bfloat16
AXES = ("gx", "gy", "gz")


def up_to(count, step):
    return -(-count // step) * step


def layer_norm(values, gain):
    average = jnp.mean(values, axis=-1, keepdims=True)
    centered = values - average
    variance = jnp.mean(centered * centered, axis=-1, keepdims=True)
    return (centered * lax.rsqrt(variance + EPSILON) * gain).astype(BF16)


def dot(left, right):
    return jnp.dot(left, right, preferred_element_type=F32)


def dot_nt(left, right):
    return lax.dot_general(left, right, (((1,), (1,)), ((), ())), preferred_element_type=F32)


def dot_tn(left, right):
    return lax.dot_general(left, right, (((0,), (0,)), ((), ())), preferred_element_type=F32)


def joined(ref, rows):
    return jnp.concatenate([ref[j, rows, :] for j in range(ref.shape[0])], axis=1)


def split_store(ref, rows, values):
    for j in range(ref.shape[0]):
        ref[j, rows, :] = values[:, j * LANES : (j + 1) * LANES]


def call(kernel, outs, *args, spaces=None, scratch=(), vmem=True, aliases=None, limit=24 << 20, work=None):
    kinds = [pltpu.VMEM(s, d) if vmem else jax.ShapeDtypeStruct(s, d) for s, d in outs]
    spaces = spaces or [pltpu.VMEM] * len(args)
    return pl.pallas_call(
        kernel,
        out_shape=kinds,
        in_specs=[pl.BlockSpec(memory_space=s) for s in spaces],
        out_specs=[pl.BlockSpec(memory_space=pltpu.VMEM) for _ in outs],
        scratch_shapes=list(scratch),
        input_output_aliases=aliases or {},
        compiler_params=pltpu.CompilerParams(vmem_limit_bytes=limit),
        cost_estimate=work and pl.CostEstimate(flops=work, bytes_accessed=0, transcendentals=0),
    )(*args)


class Sizes:
    def __init__(self, extent, channels):
        self.x, self.y, self.z = extent
        self.c = channels
        self.parts = channels // LANES
        self.cells = self.x * self.y * self.z
        self.mx, self.my, self.mz = (n // 2 for n in extent)
        self.mids = self.mx * self.my * self.mz
        self.coarse = self.mids // 8
        self.mzp = up_to(self.mz + 2, 8)
        self.fine_rows = (self.x + 2) * (self.y + 2) * self.z
        self.mid_rows = (self.mx + 2) * (self.my + 2) * self.mzp
        self.bias_rows = up_to(self.z + self.mzp + 2, 8)
        self.ones_at = self.mid_rows + self.bias_rows
        self.scale_at = self.ones_at + 4 * self.z
        self.kept_rows = self.scale_at + 8
        self.fy, self.gy = self.x * self.z, self.mx * self.mz
        self.fx, self.gx = (self.y + 2) * self.z, (self.my + 2) * self.mz
        self.fz, self.gz = (self.x + 2) * (self.y + 2), (self.mx + 2) * (self.my + 2)
        self.fzp, self.gzp = up_to(self.fz, 8), up_to(self.gz, 8)
        self.groups = [(bx, by) for bx in range(self.x // 2) for by in range(self.y // 2)]
        self.group = 4 * self.z

    def query_rows(self, bx, by):
        return [
            slice(((2 * bx + dx) * self.y + 2 * by) * self.z, ((2 * bx + dx) * self.y + 2 * by + 2) * self.z)
            for dx in (0, 1)
        ]


def pooling(size):
    x, y, z = np.unravel_index(np.arange(size.cells), (size.x, size.y, size.z))
    middle = ((x // 2) * size.my + y // 2) * size.mz + z // 2
    coarse = ((x // 4) * (size.my // 2) + y // 4) * (size.mz // 2) + z // 4
    rows = np.zeros((size.mids + size.coarse, size.cells), np.float32)
    rows[middle, np.arange(size.cells)] = 1.0
    rows[size.mids + coarse, np.arange(size.cells)] = 1.0
    grid = rows[: size.mids].reshape(size.mx, size.my, size.mz, size.cells)
    faces = [grid[:, at].reshape(size.gy, size.cells) for at in (0, size.my - 1)]
    return np.concatenate([rows, rows[size.mids :], *faces]).astype(jnp.bfloat16)


def window_bias(size):
    query_z = np.arange(size.group) % size.z

    def seen(keys, factor):
        start = 2 * (query_z // factor)
        return (keys[:, None] >= start - 1) & (keys[:, None] <= start + 2)

    place = np.arange(size.mzp)
    middle = np.where(place < size.mz, place, np.where(place == size.mz, -1, size.mz))
    held = seen(middle, 4) & (place[:, None] < size.mz + 2)
    rows = np.concatenate([seen(np.arange(size.z), 2), held, seen(np.array([-1, size.z]), 2)])
    bias = np.where(rows, 0.0, NEGATIVE).astype(np.float32)
    bias = np.concatenate([bias, np.zeros((up_to(len(bias), 8) - len(bias), size.group), np.float32)])
    rows = np.tile(np.concatenate([bias, np.eye(size.group, dtype=np.float32)]), (1, HEADS))
    return np.ascontiguousarray(rows.reshape(len(rows), -1, LANES).transpose(1, 0, 2))


def arranging(size):
    rows = np.zeros((len(size.groups) * 32, 2 * size.fzp), np.float32)
    at = 0
    for bx, by in size.groups:
        for side in range(2):
            for kx in range(4):
                for ky in range(4):
                    rows[at, side * size.fzp + (2 * bx + kx) * (size.y + 2) + 2 * by + ky] = 1.0
                    at += 1
    return rows.astype(jnp.bfloat16)


def head_mask(size):
    head = np.arange(HEADS * size.group) // size.group
    return (head[:, None] == np.arange(size.c)[None, :] // (size.c // HEADS)).astype(jnp.bfloat16)


def fetch(sources, targets, sems):
    copies = [pltpu.make_async_copy(s, t, sems.at[i]) for i, (s, t) in enumerate(zip(sources, targets))]
    for copy in copies:
        copy.start()
    return copies


def is_odd(axis):
    return lax.axis_index(axis) % 2 == 1


def first_kernel(size, devices, tokens, gain, pool, both, faces, coarse_out, cells, gain_here, pool_here, sems):
    copies = fetch((tokens, gain, pool), (cells, gain_here, pool_here), sems)
    for copy in copies[:2]:
        copy.wait()
    values = layer_norm(cells[...].astype(F32), gain_here[...])
    both[: size.cells, :] = values
    copies[2].wait()
    pooled = dot(pool_here[...], values)
    at = size.mids + 2 * size.coarse
    both[size.cells :, :] = (pooled[: size.mids] * 0.125).astype(BF16)
    pack = (pooled[size.mids : at] * (1.0 / 64.0)).astype(BF16)
    for row in range(0, devices * size.coarse, 2 * size.coarse):
        coarse_out[row : row + 2 * size.coarse, :] = pack
    face = size.fy + size.gy
    for side, y in enumerate((0, size.y - 1)):
        rows = [slice((x * size.y + y) * size.z, (x * size.y + y + 1) * size.z) for x in range(size.x)]
        cut = jnp.concatenate([values[r].astype(F32) for r in rows], axis=0)
        faces[side * face : side * face + size.fy, :] = cut.astype(BF16)
        mids = pooled[at + side * size.gy : at + (side + 1) * size.gy] * 0.125
        faces[side * face + size.fy : (side + 1) * face, :] = mids.astype(BF16)


def prepare_kernel(size, both, after, biases, head_scale, *refs):
    held = (len(refs) - 5) // 2
    sources, targets = refs[:held], refs[held : 2 * held]
    queries, fine, mid, scale_here, sems = refs[2 * held :]
    rows = mid.at[:, pl.ds(size.mid_rows, size.scale_at - size.mid_rows), :]
    copies = fetch((*sources, head_scale, biases), (*targets, scale_here, rows), sems)
    cells = both[: size.cells, :].astype(F32)
    mids = both[size.cells :, :].astype(F32)
    mid[:, : size.mid_rows, :] = jnp.zeros((size.parts, size.mid_rows, LANES), F32)
    for x in range(size.x):
        at = ((x + 1) * (size.y + 2) + 1) * size.z
        split_store(fine, slice(at, at + size.y * size.z), cells[x * size.y * size.z : (x + 1) * size.y * size.z])
    for x in range(size.mx):
        for y in range(size.my):
            at = ((x + 1) * (size.my + 2) + y + 1) * size.mzp
            row = (x * size.my + y) * size.mz
            split_store(mid, slice(at, at + size.mz), mids[row : row + size.mz])
    copies[0].wait()
    queries[...] = dot(both[: size.cells, :], targets[0][...]).astype(BF16)
    for copy in copies[1:]:
        copy.wait()
    split_store(mid, slice(size.scale_at, size.scale_at + 1), lane_scale(size, scale_here))


def pick(odd, from_a, from_b):
    first, second = from_a[...].astype(F32), from_b[...].astype(F32)
    return jnp.where(odd, first, second), jnp.where(odd, second, first)


def from_sides(size, y_refs):
    if len(y_refs) == 1:
        both = y_refs[0][...].astype(F32)
        return both[size.fy + size.gy :], both[: size.fy + size.gy]
    return y_refs[0][...].astype(F32), y_refs[1][...].astype(F32)


def x_kernel(size, both, *refs):
    y_refs, (face_a, face_b) = refs[:-2], refs[-2:]
    y_low, y_high = from_sides(size, y_refs)
    cells = both[: size.cells, :].astype(F32)
    mids = both[size.cells :, :].astype(F32)

    def cut(x, mx):
        fine_at, own = slice(x * size.z, (x + 1) * size.z), size.y * size.z
        mid_at, own_mid = slice(size.fy + mx * size.mz, size.fy + (mx + 1) * size.mz), size.my * size.mz
        return jnp.concatenate(
            [
                y_low[fine_at],
                cells[x * own : (x + 1) * own],
                y_high[fine_at],
                y_low[mid_at],
                mids[mx * own_mid : (mx + 1) * own_mid],
                y_high[mid_at],
            ],
            axis=0,
        )

    low, high = cut(0, 0), cut(size.x - 1, size.mx - 1)
    odd = is_odd("gx")
    face_a[...] = jnp.where(odd, low, high).astype(BF16)
    face_b[...] = jnp.where(odd, high, low).astype(BF16)


def z_kernel(size, fine_in, mid_in, from_a, from_b, *refs):
    y_refs, (face_a, face_b, fine, mid) = refs[:-4], refs[-4:]
    y_low, y_high = from_sides(size, y_refs)
    low, high = pick(is_odd("gx"), from_a, from_b)
    for x, halo in ((0, low), (size.x + 1, high)):
        split_store(fine, slice(x * size.fx, (x + 1) * size.fx), halo[: size.fx])
    for x, halo in ((0, low), (size.mx + 1, high)):
        for y in range(size.my + 2):
            at = (x * (size.my + 2) + y) * size.mzp
            row = size.fx + y * size.mz
            split_store(mid, slice(at, at + size.mz), halo[row : row + size.mz])
    for y, my, halo in ((0, 0, y_low), (size.y + 1, size.my + 1, y_high)):
        for x in range(size.x):
            at = ((x + 1) * (size.y + 2) + y) * size.z
            split_store(fine, slice(at, at + size.z), halo[x * size.z : (x + 1) * size.z])
        for x in range(size.mx):
            at = ((x + 1) * (size.my + 2) + my) * size.mzp
            row = size.fy + x * size.mz
            split_store(mid, slice(at, at + size.mz), halo[row : row + size.mz])

    def cut(z, mz):
        parts = [
            joined(fine, pl.ds(z, size.fz, stride=size.z)),
            jnp.zeros((size.fzp - size.fz, size.c), F32),
            joined(mid, pl.ds(mz, size.gz, stride=size.mzp)),
            jnp.zeros((size.gzp - size.gz, size.c), F32),
        ]
        return jnp.concatenate([p for p in parts if p.shape[0]], axis=0)

    below, above = cut(0, 0), cut(size.z - 1, size.mz - 1)
    odd = is_odd("gz")
    face_a[...] = jnp.where(odd, below, above).astype(BF16)
    face_b[...] = jnp.where(odd, above, below).astype(BF16)


def lane_scale(size, head_scale):
    factor = LOG2E / math.sqrt(size.c // HEADS)
    return jnp.concatenate([jnp.full((1, size.group), head_scale[h] * factor, F32) for h in range(HEADS)], axis=1)


def spread_queries(size, queries, rows, mask):
    some = jnp.concatenate([queries[r, :] for r in rows], axis=0)
    return jnp.concatenate([some] * HEADS, axis=0) * mask


def soft(scores):
    weights = jnp.exp2(scores - jnp.max(scores, axis=0, keepdims=True))
    return (weights * (1.0 / jnp.sum(weights, axis=0, keepdims=True))).astype(BF16)


def tiled(scores, one):
    length = one.shape[0]
    return (scores.reshape(-1, length, scores.shape[-1]) + one[None]).reshape(scores.shape)


def gather_heads(size, total, wide):
    return jnp.sum(total.reshape(HEADS, size.group, size.c) * wide, axis=0)


def own_kernel(
    size, kept, queries, fine, coarse, key_weight, value_weight, mask, coarse_out, fine_out, stats
):
    block = joined(fine, slice(None)).astype(BF16)
    keys = dot(block, key_weight[...]).astype(BF16)
    values = dot(block, value_weight[...]).astype(BF16)
    cells = coarse[...]
    coarse_keys = dot(cells, key_weight[...]).astype(BF16)
    coarse_values = dot(cells, value_weight[...]).astype(BF16)
    scale = joined(kept, slice(size.scale_at, size.scale_at + 1))
    spread_mask = mask[...]
    wide = spread_mask.astype(F32).reshape(HEADS, size.group, size.c)
    run_bias = joined(kept, slice(size.mid_rows, size.mid_rows + size.z))
    fine_row = (size.y + 2) * size.z
    for index, (bx, by) in enumerate(size.groups):
        at = slice(index * size.group, (index + 1) * size.group)
        spread = spread_queries(size, queries, size.query_rows(bx, by), spread_mask)
        total = dot_tn(soft(dot_nt(coarse_keys, spread) * scale), coarse_values)
        coarse_out[at, :] = gather_heads(size, total, wide)
        slabs = [
            slice((2 * bx + k) * fine_row + 2 * by * size.z, (2 * bx + k) * fine_row + (2 * by + 4) * size.z)
            for k in range(4)
        ]
        some_keys = jnp.concatenate([keys[s] for s in slabs], axis=0)
        some_values = jnp.concatenate([values[s] for s in slabs], axis=0)
        scores = tiled(dot_nt(some_keys, spread) * scale, run_bias)
        highest = jnp.max(scores, axis=0, keepdims=True)
        weights = jnp.exp2(scores - highest)
        stats[index : index + 1, :] = highest
        stats[len(size.groups) + index : len(size.groups) + index + 1, :] = jnp.sum(weights, axis=0, keepdims=True)
        fine_out[at, :] = gather_heads(size, dot_tn(weights.astype(BF16), some_values), wide)


def last_kernel(
    size,
    tokens,
    mlp_gain,
    out_weight,
    up_weight,
    down_weight,
    queries,
    mid_in,
    from_a,
    from_b,
    coarse_out,
    fine_out,
    stats,
    key_weight,
    value_weight,
    mask,
    arrange,
    out,
    mid,
    attended,
    joint,
    factors,
    tokens_here,
    gain_here,
    out_here,
    up_here,
    down_here,
    sems,
):
    copies = fetch(
        (tokens, mlp_gain, out_weight, up_weight, down_weight),
        (tokens_here, gain_here, out_here, up_here, down_here),
        sems,
    )
    low, high = pick(is_odd("gz"), from_a, from_b)
    mid[...] = mid_in[:, : size.mid_rows, :]
    split_store(mid, pl.ds(size.mz, size.gz, stride=size.mzp), low[size.fzp : size.fzp + size.gz])
    split_store(mid, pl.ds(size.mz + 1, size.gz, stride=size.mzp), high[size.fzp : size.fzp + size.gz])
    ends = jnp.concatenate([low[: size.fzp], high[: size.fzp]], axis=0).astype(BF16)
    ends = dot(arrange[...], ends).astype(BF16)
    mids = joined(mid, slice(None)).astype(BF16)
    cells = jnp.concatenate([ends, mids], axis=0)
    keys = dot(cells, key_weight[...]).astype(BF16)
    values = dot(cells, value_weight[...]).astype(BF16)
    scale = joined(mid_in, slice(size.scale_at, size.scale_at + 1))
    spread_mask = mask[...]
    wide = spread_mask.astype(F32).reshape(HEADS, size.group, size.c)
    bias = joined(mid_in, slice(size.mid_rows + size.z, size.ones_at))
    mid_bias, low_bias, high_bias = bias[: size.mzp], bias[size.mzp : size.mzp + 1], bias[size.mzp + 1 : size.mzp + 2]
    ones = joined(mid_in, slice(size.ones_at, size.scale_at))
    mid_row = (size.my + 2) * size.mzp
    count = len(size.groups)

    for index, (bx, by) in enumerate(size.groups):
        at = slice(index * size.group, (index + 1) * size.group)
        spread = spread_queries(size, queries, size.query_rows(bx, by), spread_mask)
        ends_at = slice(32 * index, 32 * index + 32)
        start = [
            count * 32 + (2 * (bx // 2) + k) * mid_row + 2 * (by // 2) * size.mzp for k in range(4)
        ]
        slabs = [ends_at] + [slice(s, s + 4 * size.mzp) for s in start]
        both = dot_nt(jnp.concatenate([keys[s] for s in slabs], axis=0), spread) * scale
        scores = jnp.concatenate([both[:16] + low_bias, both[16:32] + high_bias], axis=0)
        before = stats[index : index + 1, :]
        highest = jnp.maximum(before, jnp.max(scores, axis=0, keepdims=True))
        weights = jnp.exp2(scores - highest)
        shrink = jnp.exp2(before - highest)
        summed = stats[count + index : count + index + 1, :] * shrink + jnp.sum(weights, axis=0, keepdims=True)
        inverse = 1.0 / summed
        factor = ones * (shrink * inverse)
        coarser = factor.astype(BF16)
        factors[at, :] = coarser
        finer = slice(count * size.group + at.start, count * size.group + at.stop)
        factors[finer, :] = (factor - coarser.astype(F32)).astype(BF16)
        weights = jnp.concatenate([(weights * inverse).astype(BF16), soft(tiled(both[32:], mid_bias))], axis=0)
        total = dot_tn(weights, jnp.concatenate([values[s] for s in slabs], axis=0))
        joint[at, :] = gather_heads(size, total, wide) + coarse_out[at, :]

    spread_factors = dot(factors[...], spread_mask)
    half = count * size.group
    result = joint[...] + fine_out[...] * (spread_factors[:half] + spread_factors[half:])
    for index, (bx, by) in enumerate(size.groups):
        part = result[index * size.group : (index + 1) * size.group].astype(BF16)
        for k, r in enumerate(size.query_rows(bx, by)):
            attended[r, :] = part[k * 2 * size.z : (k + 1) * 2 * size.z]
    for copy in copies:
        copy.wait()
    residual = (tokens_here[...].astype(F32) + dot(attended[...], out_here[...])).astype(BF16)
    second = layer_norm(residual.astype(F32), gain_here[...])
    hidden = jax.nn.gelu(dot(second, up_here[...]), approximate=True).astype(BF16)
    out[...] = (residual.astype(F32) + dot(hidden, down_here[...])).astype(BF16)


def swap(array, axis, start):
    count = lax.axis_size(axis)
    pairs = []
    for i in range(start, count, 2):
        other = (i + 1) % count
        pairs += [(i, other), (other, i)]
    return lax.ppermute(array, axis, pairs)


def shift(array, axis, by):
    count = lax.axis_size(axis)
    return lax.ppermute(array, axis, [(i, (i + by) % count) for i in range(count)])


def shards(
    tokens,
    norm_gain,
    query_weight,
    key_weight,
    value_weight,
    head_scale,
    out_weight,
    mlp_gain,
    up_weight,
    down_weight,
):
    channels = tokens.shape[-1]
    size = Sizes(tokens.shape[:3], channels)
    devices = math.prod(lax.axis_size(a) for a in AXES)
    fx, gx, fy, gy = size.fx, size.gx, size.fy, size.gy
    face_z = size.fzp + size.gzp
    smem, vmem, hbm = pltpu.SMEM, pltpu.VMEM, pltpu.HBM

    def pinned(*arrays):
        return [pltpu.with_memory_space_constraint(jnp.asarray(a), hbm) for a in arrays]

    flat, gain, gain_mlp, scales = pinned(
        tokens.reshape(size.cells, channels), norm_gain.reshape(1, -1), mlp_gain.reshape(1, -1), head_scale
    )
    biases, pool = pinned(window_bias(size), pooling(size))
    both, faces, coarse = call(
        functools.partial(first_kernel, size, devices),
        [
            ((size.cells + size.mids, channels), BF16),
            ((2 * (fy + gy), channels), BF16),
            ((devices * size.coarse, channels), BF16),
        ],
        flat,
        gain,
        pool,
        spaces=[hbm] * 3,
        scratch=[
            pltpu.VMEM(flat.shape, BF16),
            pltpu.VMEM(gain.shape, F32),
            pltpu.VMEM(pool.shape, BF16),
            pltpu.SemaphoreType.DMA((3,)),
        ],
    )
    if lax.axis_size("gy") == 2:
        from_y = [swap(faces, "gy", 0)]
    else:
        from_y = [shift(faces[fy + gy :], "gy", 1), shift(faces[: fy + gy], "gy", -1)]
    gathered = lax.all_to_all(coarse.reshape(devices, size.coarse, channels), AXES, 0, 0).reshape(-1, channels)
    face_a, face_b = call(
        functools.partial(x_kernel, size),
        [((fx + gx, channels), BF16), ((fx + gx, channels), BF16)],
        both,
        *from_y,
        work=20_000_000_000,
    )
    from_a = swap(face_a, "gx", 0)
    from_b = swap(face_b, "gx", 1)
    held = pinned(
        query_weight,
        key_weight,
        value_weight,
        head_mask(size),
        arranging(size),
    )
    late = pinned(out_weight, up_weight, down_weight)
    *weights, queries, fine, mid = call(
        functools.partial(prepare_kernel, size),
        [(a.shape, a.dtype) for a in held]
        + [
            ((size.cells, channels), BF16),
            ((size.parts, size.fine_rows, LANES), F32),
            ((size.parts, size.kept_rows, LANES), F32),
        ],
        both,
        face_a,
        biases,
        scales,
        *held,
        spaces=[vmem] * 2 + [hbm] * (2 + len(held)),
        scratch=[pltpu.SMEM((HEADS,), F32), pltpu.SemaphoreType.DMA((2 + len(held),))],
    )
    wq, wk, wv, mask, arrange = weights
    z_a, z_b, fine, mid = call(
        functools.partial(z_kernel, size),
        [
            ((face_z, channels), BF16),
            ((face_z, channels), BF16),
            ((size.parts, size.fine_rows, LANES), F32),
            ((size.parts, size.kept_rows, LANES), F32),
        ],
        fine,
        mid,
        from_a,
        from_b,
        *from_y,
        aliases={0: 2, 1: 3},
    )
    got_a = swap(z_a, "gz", 0)
    got_b = swap(z_b, "gz", 1)
    lanes = HEADS * size.group
    coarse_out, fine_out, stats = call(
        functools.partial(own_kernel, size),
        [
            ((size.cells, channels), F32),
            ((size.cells, channels), F32),
            ((2 * len(size.groups), lanes), F32),
        ],
        mid,
        queries,
        fine,
        gathered,
        wk,
        wv,
        mask,
    )
    out = call(
        functools.partial(last_kernel, size),
        [((size.cells, channels), BF16)],
        flat,
        gain_mlp,
        *late,
        queries,
        mid,
        got_a,
        got_b,
        coarse_out,
        fine_out,
        stats,
        wk,
        wv,
        mask,
        arrange,
        spaces=[hbm] * 5 + [vmem] * 11,
        scratch=[
            pltpu.VMEM((size.parts, size.mid_rows, LANES), F32),
            pltpu.VMEM((size.cells, channels), BF16),
            pltpu.VMEM((size.cells, channels), F32),
            pltpu.VMEM((2 * size.cells, lanes), BF16),
            pltpu.VMEM(flat.shape, BF16),
            pltpu.VMEM(gain_mlp.shape, F32),
            *[pltpu.VMEM(a.shape, BF16) for a in late],
            pltpu.SemaphoreType.DMA((5,)),
        ],
        vmem=False,
    )[0]
    return out.reshape(tokens.shape)


def solution(mesh):
    in_specs = (P("gx", "gy", "gz", None), P(), P(), P(), P(), P(), P(), P(), P(), P())
    out_specs = P("gx", "gy", "gz", None)
    return jax.shard_map(shards, mesh=mesh, in_specs=in_specs, out_specs=out_specs, check_vma=False)
```

```python
import functools
import math

import jax
import jax.numpy as jnp
import numpy as np
from jax import lax
from jax.experimental import pallas as pl
from jax.experimental.pallas import tpu as pltpu
from jax.sharding import PartitionSpec as P

HEADS = 8
EPSILON = 1e-05
LOG2E = 1.4426950408889634
NEGATIVE = -1e30
LANES = 128
F32 = jnp.float32
BF16 = jnp.bfloat16
AXES = ("gx", "gy", "gz")


def up_to(count, step):
    return -(-count // step) * step


def layer_norm(values, gain):
    average = jnp.mean(values, axis=-1, keepdims=True)
    centered = values - average
    variance = jnp.mean(centered * centered, axis=-1, keepdims=True)
    return (centered * lax.rsqrt(variance + EPSILON) * gain).astype(BF16)


def dot(left, right):
    return jnp.dot(left, right, preferred_element_type=F32)


def dot_nt(left, right):
    return lax.dot_general(left, right, (((1,), (1,)), ((), ())), preferred_element_type=F32)


def dot_tn(left, right):
    return lax.dot_general(left, right, (((0,), (0,)), ((), ())), preferred_element_type=F32)


def joined(ref, rows):
    return jnp.concatenate([ref[j, rows, :] for j in range(ref.shape[0])], axis=1)


def split_store(ref, rows, values):
    for j in range(ref.shape[0]):
        ref[j, rows, :] = values[:, j * LANES : (j + 1) * LANES]


def call(kernel, outs, *args, spaces=None, scratch=(), vmem=True, aliases=None, limit=24 << 20, work=None):
    kinds = [pltpu.VMEM(s, d) if vmem else jax.ShapeDtypeStruct(s, d) for s, d in outs]
    spaces = spaces or [pltpu.VMEM] * len(args)
    return pl.pallas_call(
        kernel,
        out_shape=kinds,
        in_specs=[pl.BlockSpec(memory_space=s) for s in spaces],
        out_specs=[pl.BlockSpec(memory_space=pltpu.VMEM) for _ in outs],
        scratch_shapes=list(scratch),
        input_output_aliases=aliases or {},
        compiler_params=pltpu.CompilerParams(vmem_limit_bytes=limit),
        cost_estimate=work and pl.CostEstimate(flops=work, bytes_accessed=0, transcendentals=0),
    )(*args)


class Sizes:
    def __init__(self, extent, channels):
        self.x, self.y, self.z = extent
        self.c = channels
        self.parts = channels // LANES
        self.cells = self.x * self.y * self.z
        self.mx, self.my, self.mz = (n // 2 for n in extent)
        self.mids = self.mx * self.my * self.mz
        self.coarse = self.mids // 8
        self.mzp = up_to(self.mz + 2, 8)
        self.fine_rows = (self.x + 2) * (self.y + 2) * self.z
        self.mid_rows = (self.mx + 2) * (self.my + 2) * self.mzp
        self.bias_rows = up_to(self.z + self.mzp + 2, 8)
        self.ones_at = self.mid_rows + self.bias_rows
        self.scale_at = self.ones_at + 4 * self.z
        self.kept_rows = self.scale_at + 8
        self.fy, self.gy = self.x * self.z, self.mx * self.mz
        self.fx, self.gx = (self.y + 2) * self.z, (self.my + 2) * self.mz
        self.fz, self.gz = (self.x + 2) * (self.y + 2), (self.mx + 2) * (self.my + 2)
        self.fzp, self.gzp = self.fz, self.gz
        self.groups = [(bx, by) for bx in range(self.x // 2) for by in range(self.y // 2)]
        self.group = 4 * self.z

    def query_rows(self, bx, by):
        return [
            slice(((2 * bx + dx) * self.y + 2 * by) * self.z, ((2 * bx + dx) * self.y + 2 * by + 2) * self.z)
            for dx in (0, 1)
        ]


def pooling(size):
    x, y, z = np.unravel_index(np.arange(size.cells), (size.x, size.y, size.z))
    middle = ((x // 2) * size.my + y // 2) * size.mz + z // 2
    coarse = ((x // 4) * (size.my // 2) + y // 4) * (size.mz // 2) + z // 4
    rows = np.zeros((size.mids + size.coarse, size.cells), np.float32)
    rows[middle, np.arange(size.cells)] = 1.0
    rows[size.mids + coarse, np.arange(size.cells)] = 1.0
    grid = rows[: size.mids].reshape(size.mx, size.my, size.mz, size.cells)
    faces = [grid[:, at].reshape(size.gy, size.cells) for at in (0, size.my - 1)]
    return np.concatenate([rows, rows[size.mids :], *faces]).astype(jnp.bfloat16)


def window_bias(size):
    query_z = np.arange(size.group) % size.z

    def seen(keys, factor):
        start = 2 * (query_z // factor)
        return (keys[:, None] >= start - 1) & (keys[:, None] <= start + 2)

    place = np.arange(size.mzp)
    middle = np.where(place < size.mz, place, np.where(place == size.mz, -1, size.mz))
    held = seen(middle, 4) & (place[:, None] < size.mz + 2)
    rows = np.concatenate([seen(np.arange(size.z), 2), held, seen(np.array([-1, size.z]), 2)])
    bias = np.where(rows, 0.0, NEGATIVE).astype(np.float32)
    bias = np.concatenate([bias, np.zeros((up_to(len(bias), 8) - len(bias), size.group), np.float32)])
    rows = np.tile(np.concatenate([bias, np.eye(size.group, dtype=np.float32)]), (1, HEADS))
    return np.ascontiguousarray(rows.reshape(len(rows), -1, LANES).transpose(1, 0, 2))


def arranging(size):
    rows = np.zeros((len(size.groups) * 32, 2 * size.fzp), np.float32)
    at = 0
    for bx, by in size.groups:
        for side in range(2):
            for kx in range(4):
                for ky in range(4):
                    rows[at, side * size.fzp + (2 * bx + kx) * (size.y + 2) + 2 * by + ky] = 1.0
                    at += 1
    return rows.astype(jnp.bfloat16)


def head_mask(size):
    head = np.arange(HEADS * size.group) // size.group
    return (head[:, None] == np.arange(size.c)[None, :] // (size.c // HEADS)).astype(jnp.bfloat16)


def fetch(sources, targets, sems):
    copies = [pltpu.make_async_copy(s, t, sems.at[i]) for i, (s, t) in enumerate(zip(sources, targets))]
    for copy in copies:
        copy.start()
    return copies


def is_odd(axis):
    return lax.axis_index(axis) % 2 == 1


def first_kernel(size, devices, tokens, gain, pool, both, faces, coarse_out, cells, gain_here, pool_here, sems):
    copies = fetch((tokens, gain, pool), (cells, gain_here, pool_here), sems)
    for copy in copies[:2]:
        copy.wait()
    values = layer_norm(cells[...].astype(F32), gain_here[...])
    both[: size.cells, :] = values
    copies[2].wait()
    pooled = dot(pool_here[...], values)
    at = size.mids + 2 * size.coarse
    both[size.cells :, :] = (pooled[: size.mids] * 0.125).astype(BF16)
    pack = (pooled[size.mids : at] * (1.0 / 64.0)).astype(BF16)
    for row in range(0, devices * size.coarse, 2 * size.coarse):
        coarse_out[row : row + 2 * size.coarse, :] = pack
    face = size.fy + size.gy
    for side, y in enumerate((0, size.y - 1)):
        rows = [slice((x * size.y + y) * size.z, (x * size.y + y + 1) * size.z) for x in range(size.x)]
        cut = jnp.concatenate([values[r].astype(F32) for r in rows], axis=0)
        faces[side * face : side * face + size.fy, :] = cut.astype(BF16)
        mids = pooled[at + side * size.gy : at + (side + 1) * size.gy] * 0.125
        faces[side * face + size.fy : (side + 1) * face, :] = mids.astype(BF16)


def prepare_kernel(size, both, after, biases, head_scale, *refs):
    held = (len(refs) - 5) // 2
    sources, targets = refs[:held], refs[held : 2 * held]
    queries, fine, mid, scale_here, sems = refs[2 * held :]
    rows = mid.at[:, pl.ds(size.mid_rows, size.scale_at - size.mid_rows), :]
    copies = fetch((*sources, head_scale, biases), (*targets, scale_here, rows), sems)
    cells = both[: size.cells, :].astype(F32)
    mids = both[size.cells :, :].astype(F32)
    mid[:, : size.mid_rows, :] = jnp.zeros((size.parts, size.mid_rows, LANES), F32)
    for x in range(size.x):
        at = ((x + 1) * (size.y + 2) + 1) * size.z
        split_store(fine, slice(at, at + size.y * size.z), cells[x * size.y * size.z : (x + 1) * size.y * size.z])
    for x in range(size.mx):
        for y in range(size.my):
            at = ((x + 1) * (size.my + 2) + y + 1) * size.mzp
            row = (x * size.my + y) * size.mz
            split_store(mid, slice(at, at + size.mz), mids[row : row + size.mz])
    copies[0].wait()
    queries[...] = dot(both[: size.cells, :], targets[0][...]).astype(BF16)
    for copy in copies[1:]:
        copy.wait()
    split_store(mid, slice(size.scale_at, size.scale_at + 1), lane_scale(size, scale_here))


def pick(odd, from_a, from_b):
    first, second = from_a[...].astype(F32), from_b[...].astype(F32)
    return jnp.where(odd, first, second), jnp.where(odd, second, first)


def from_sides(size, y_refs):
    if len(y_refs) == 1:
        both = y_refs[0][...].astype(F32)
        return both[size.fy + size.gy :], both[: size.fy + size.gy]
    return y_refs[0][...].astype(F32), y_refs[1][...].astype(F32)


def x_kernel(size, both, *refs):
    y_refs, (face_a, face_b) = refs[:-2], refs[-2:]
    y_low, y_high = from_sides(size, y_refs)
    cells = both[: size.cells, :].astype(F32)
    mids = both[size.cells :, :].astype(F32)

    def cut(x, mx):
        fine_at, own = slice(x * size.z, (x + 1) * size.z), size.y * size.z
        mid_at, own_mid = slice(size.fy + mx * size.mz, size.fy + (mx + 1) * size.mz), size.my * size.mz
        return jnp.concatenate(
            [
                y_low[fine_at],
                cells[x * own : (x + 1) * own],
                y_high[fine_at],
                y_low[mid_at],
                mids[mx * own_mid : (mx + 1) * own_mid],
                y_high[mid_at],
            ],
            axis=0,
        )

    low, high = cut(0, 0), cut(size.x - 1, size.mx - 1)
    odd = is_odd("gx")
    face_a[...] = jnp.where(odd, low, high).astype(BF16)
    face_b[...] = jnp.where(odd, high, low).astype(BF16)


def z_kernel(size, fine_in, mid_in, from_a, from_b, *refs):
    y_refs, (face_a, face_b, fine, mid) = refs[:-4], refs[-4:]
    y_low, y_high = from_sides(size, y_refs)
    low, high = pick(is_odd("gx"), from_a, from_b)
    for x, halo in ((0, low), (size.x + 1, high)):
        split_store(fine, slice(x * size.fx, (x + 1) * size.fx), halo[: size.fx])
    for x, halo in ((0, low), (size.mx + 1, high)):
        for y in range(size.my + 2):
            at = (x * (size.my + 2) + y) * size.mzp
            row = size.fx + y * size.mz
            split_store(mid, slice(at, at + size.mz), halo[row : row + size.mz])
    for y, my, halo in ((0, 0, y_low), (size.y + 1, size.my + 1, y_high)):
        for x in range(size.x):
            at = ((x + 1) * (size.y + 2) + y) * size.z
            split_store(fine, slice(at, at + size.z), halo[x * size.z : (x + 1) * size.z])
        for x in range(size.mx):
            at = ((x + 1) * (size.my + 2) + my) * size.mzp
            row = size.fy + x * size.mz
            split_store(mid, slice(at, at + size.mz), halo[row : row + size.mz])

    def cut(z, mz):
        parts = [
            joined(fine, pl.ds(z, size.fz, stride=size.z)),
            jnp.zeros((size.fzp - size.fz, size.c), F32),
            joined(mid, pl.ds(mz, size.gz, stride=size.mzp)),
            jnp.zeros((size.gzp - size.gz, size.c), F32),
        ]
        return jnp.concatenate([p for p in parts if p.shape[0]], axis=0)

    below, above = cut(0, 0), cut(size.z - 1, size.mz - 1)
    odd = is_odd("gz")
    face_a[...] = jnp.where(odd, below, above).astype(BF16)
    face_b[...] = jnp.where(odd, above, below).astype(BF16)


def lane_scale(size, head_scale):
    factor = LOG2E / math.sqrt(size.c // HEADS)
    return jnp.concatenate([jnp.full((1, size.group), head_scale[h] * factor, F32) for h in range(HEADS)], axis=1)


def spread_queries(size, queries, rows, mask):
    some = jnp.concatenate([queries[r, :] for r in rows], axis=0)
    return jnp.concatenate([some] * HEADS, axis=0) * mask


def soft(scores):
    weights = jnp.exp2(scores - jnp.max(scores, axis=0, keepdims=True))
    return (weights * (1.0 / jnp.sum(weights, axis=0, keepdims=True))).astype(BF16)


def tiled(scores, one):
    length = one.shape[0]
    return (scores.reshape(-1, length, scores.shape[-1]) + one[None]).reshape(scores.shape)


def gather_heads(size, total):
    heads, width = HEADS // size.parts, size.c // HEADS
    lane = lax.broadcasted_iota(jnp.int32, (size.group, LANES), 1)
    parts = []
    for j in range(size.parts):
        blocks = [
            total[(j * heads + h) * size.group : (j * heads + h + 1) * size.group, j * LANES : (j + 1) * LANES]
            for h in range(heads)
        ]
        result = blocks[0]
        for h in range(1, heads):
            result = jnp.where(lane >= h * width, blocks[h], result)
        parts.append(result)
    return jnp.concatenate(parts, axis=1)


def own_kernel(
    size, kept, queries, fine, coarse, key_weight, value_weight, mask, coarse_out, fine_out, stats
):
    block = joined(fine, slice(None)).astype(BF16)
    keys = dot(block, key_weight[...]).astype(BF16)
    values = dot(block, value_weight[...]).astype(BF16)
    cells = coarse[...]
    coarse_keys = dot(cells, key_weight[...]).astype(BF16)
    coarse_values = dot(cells, value_weight[...]).astype(BF16)
    scale = joined(kept, slice(size.scale_at, size.scale_at + 1))
    spread_mask = mask[...]
    run_bias = joined(kept, slice(size.mid_rows, size.mid_rows + size.z))
    fine_row = (size.y + 2) * size.z
    for index, (bx, by) in enumerate(size.groups):
        at = slice(index * size.group, (index + 1) * size.group)
        spread = spread_queries(size, queries, size.query_rows(bx, by), spread_mask)
        total = dot_tn(soft(dot_nt(coarse_keys, spread) * scale), coarse_values)
        coarse_out[at, :] = gather_heads(size, total)
        slabs = [
            slice((2 * bx + k) * fine_row + 2 * by * size.z, (2 * bx + k) * fine_row + (2 * by + 4) * size.z)
            for k in range(4)
        ]
        some_keys = jnp.concatenate([keys[s] for s in slabs], axis=0)
        some_values = jnp.concatenate([values[s] for s in slabs], axis=0)
        scores = tiled(dot_nt(some_keys, spread) * scale, run_bias)
        highest = jnp.max(scores, axis=0, keepdims=True)
        weights = jnp.exp2(scores - highest)
        stats[index : index + 1, :] = highest
        stats[len(size.groups) + index : len(size.groups) + index + 1, :] = jnp.sum(weights, axis=0, keepdims=True)
        fine_out[at, :] = gather_heads(size, dot_tn(weights.astype(BF16), some_values))


def weigh_heads(size, total, wide):
    heads = HEADS // size.parts
    parts = []
    for j in range(size.parts):
        rows = slice(j * heads * size.group, (j + 1) * heads * size.group)
        cut = total[rows, j * LANES : (j + 1) * LANES].reshape(heads, size.group, LANES)
        parts.append(jnp.sum(cut * wide[:heads, :, :LANES], axis=0))
    return jnp.concatenate(parts, axis=1)


def last_kernel(
    size,
    tokens,
    mlp_gain,
    out_weight,
    up_weight,
    down_weight,
    queries,
    mid_in,
    from_a,
    from_b,
    coarse_out,
    fine_out,
    stats,
    key_weight,
    value_weight,
    mask,
    arrange,
    out,
    mid,
    attended,
    joint,
    factors,
    tokens_here,
    gain_here,
    out_here,
    up_here,
    down_here,
    sems,
):
    copies = fetch(
        (tokens, mlp_gain, out_weight, up_weight, down_weight),
        (tokens_here, gain_here, out_here, up_here, down_here),
        sems,
    )
    low, high = pick(is_odd("gz"), from_a, from_b)
    mid[...] = mid_in[:, : size.mid_rows, :]
    split_store(mid, pl.ds(size.mz, size.gz, stride=size.mzp), low[size.fzp : size.fzp + size.gz])
    split_store(mid, pl.ds(size.mz + 1, size.gz, stride=size.mzp), high[size.fzp : size.fzp + size.gz])
    ends = jnp.concatenate([low[: size.fzp], high[: size.fzp]], axis=0).astype(BF16)
    ends = dot(arrange[...], ends).astype(BF16)
    mids = joined(mid, slice(None)).astype(BF16)
    cells = jnp.concatenate([ends, mids], axis=0)
    keys = dot(cells, key_weight[...]).astype(BF16)
    values = dot(cells, value_weight[...]).astype(BF16)
    scale = joined(mid_in, slice(size.scale_at, size.scale_at + 1))
    spread_mask = mask[...]
    wide = spread_mask.astype(F32).reshape(HEADS, size.group, size.c)
    bias = joined(mid_in, slice(size.mid_rows + size.z, size.ones_at))
    mid_bias, low_bias, high_bias = bias[: size.mzp], bias[size.mzp : size.mzp + 1], bias[size.mzp + 1 : size.mzp + 2]
    ones = joined(mid_in, slice(size.ones_at, size.scale_at))
    mid_row = (size.my + 2) * size.mzp
    count = len(size.groups)

    for index, (bx, by) in enumerate(size.groups):
        at = slice(index * size.group, (index + 1) * size.group)
        spread = spread_queries(size, queries, size.query_rows(bx, by), spread_mask)
        ends_at = slice(32 * index, 32 * index + 32)
        start = [
            count * 32 + (2 * (bx // 2) + k) * mid_row + 2 * (by // 2) * size.mzp for k in range(4)
        ]
        slabs = [ends_at] + [slice(s, s + 4 * size.mzp) for s in start]
        both = dot_nt(jnp.concatenate([keys[s] for s in slabs], axis=0), spread) * scale
        scores = jnp.concatenate([both[:16] + low_bias, both[16:32] + high_bias], axis=0)
        before = stats[index : index + 1, :]
        highest = jnp.maximum(before, jnp.max(scores, axis=0, keepdims=True))
        weights = jnp.exp2(scores - highest)
        shrink = jnp.exp2(before - highest)
        summed = stats[count + index : count + index + 1, :] * shrink + jnp.sum(weights, axis=0, keepdims=True)
        inverse = 1.0 / summed
        factor = ones * (shrink * inverse)
        coarser = factor.astype(BF16)
        factors[at, :] = coarser
        finer = slice(count * size.group + at.start, count * size.group + at.stop)
        factors[finer, :] = (factor - coarser.astype(F32)).astype(BF16)
        weights = jnp.concatenate([(weights * inverse).astype(BF16), soft(tiled(both[32:], mid_bias))], axis=0)
        total = dot_tn(weights, jnp.concatenate([values[s] for s in slabs], axis=0))
        joint[at, :] = weigh_heads(size, total, wide) + coarse_out[at, :]

    spread_factors = dot(factors[...], spread_mask)
    half = count * size.group
    result = joint[...] + fine_out[...] * (spread_factors[:half] + spread_factors[half:])
    for index, (bx, by) in enumerate(size.groups):
        part = result[index * size.group : (index + 1) * size.group].astype(BF16)
        for k, r in enumerate(size.query_rows(bx, by)):
            attended[r, :] = part[k * 2 * size.z : (k + 1) * 2 * size.z]
    for copy in copies:
        copy.wait()
    residual = (tokens_here[...].astype(F32) + dot(attended[...], out_here[...])).astype(BF16)
    second = layer_norm(residual.astype(F32), gain_here[...])
    hidden = jax.nn.gelu(dot(second, up_here[...]), approximate=True).astype(BF16)
    out[...] = (residual.astype(F32) + dot(hidden, down_here[...])).astype(BF16)


def swap(array, axis, start):
    count = lax.axis_size(axis)
    pairs = []
    for i in range(start, count, 2):
        other = (i + 1) % count
        pairs += [(i, other), (other, i)]
    return lax.ppermute(array, axis, pairs)


def shift(array, axis, by):
    count = lax.axis_size(axis)
    return lax.ppermute(array, axis, [(i, (i + by) % count) for i in range(count)])


def shards(
    tokens,
    norm_gain,
    query_weight,
    key_weight,
    value_weight,
    head_scale,
    out_weight,
    mlp_gain,
    up_weight,
    down_weight,
):
    channels = tokens.shape[-1]
    size = Sizes(tokens.shape[:3], channels)
    devices = math.prod(lax.axis_size(a) for a in AXES)
    fx, gx, fy, gy = size.fx, size.gx, size.fy, size.gy
    face_z = size.fzp + size.gzp
    smem, vmem, hbm = pltpu.SMEM, pltpu.VMEM, pltpu.HBM

    def pinned(*arrays):
        return [pltpu.with_memory_space_constraint(jnp.asarray(a), hbm) for a in arrays]

    flat, gain, gain_mlp, scales = pinned(
        tokens.reshape(size.cells, channels), norm_gain.reshape(1, -1), mlp_gain.reshape(1, -1), head_scale
    )
    biases, pool = pinned(window_bias(size), pooling(size))
    both, faces, coarse = call(
        functools.partial(first_kernel, size, devices),
        [
            ((size.cells + size.mids, channels), BF16),
            ((2 * (fy + gy), channels), BF16),
            ((devices * size.coarse, channels), BF16),
        ],
        flat,
        gain,
        pool,
        spaces=[hbm] * 3,
        scratch=[
            pltpu.VMEM(flat.shape, BF16),
            pltpu.VMEM(gain.shape, F32),
            pltpu.VMEM(pool.shape, BF16),
            pltpu.SemaphoreType.DMA((3,)),
        ],
    )
    if lax.axis_size("gy") == 2:
        from_y = [swap(faces, "gy", 0)]
    else:
        from_y = [shift(faces[fy + gy :], "gy", 1), shift(faces[: fy + gy], "gy", -1)]
    gathered = lax.all_to_all(coarse.reshape(devices, size.coarse, channels), AXES, 0, 0).reshape(-1, channels)
    face_a, face_b = call(
        functools.partial(x_kernel, size),
        [((fx + gx, channels), BF16), ((fx + gx, channels), BF16)],
        both,
        *from_y,
        work=20_000_000_000,
    )
    from_a = swap(face_a, "gx", 0)
    from_b = swap(face_b, "gx", 1)
    held = pinned(
        query_weight,
        key_weight,
        value_weight,
        head_mask(size),
        arranging(size),
    )
    late = pinned(out_weight, up_weight, down_weight)
    *weights, queries, fine, mid = call(
        functools.partial(prepare_kernel, size),
        [(a.shape, a.dtype) for a in held]
        + [
            ((size.cells, channels), BF16),
            ((size.parts, size.fine_rows, LANES), F32),
            ((size.parts, size.kept_rows, LANES), F32),
        ],
        both,
        face_a,
        biases,
        scales,
        *held,
        spaces=[vmem] * 2 + [hbm] * (2 + len(held)),
        scratch=[pltpu.SMEM((HEADS,), F32), pltpu.SemaphoreType.DMA((2 + len(held),))],
    )
    wq, wk, wv, mask, arrange = weights
    z_a, z_b, fine, mid = call(
        functools.partial(z_kernel, size),
        [
            ((face_z, channels), BF16),
            ((face_z, channels), BF16),
            ((size.parts, size.fine_rows, LANES), F32),
            ((size.parts, size.kept_rows, LANES), F32),
        ],
        fine,
        mid,
        from_a,
        from_b,
        *from_y,
        aliases={0: 2, 1: 3},
    )
    got_a = swap(z_a, "gz", 0)
    got_b = swap(z_b, "gz", 1)
    lanes = HEADS * size.group
    coarse_out, fine_out, stats = call(
        functools.partial(own_kernel, size),
        [
            ((size.cells, channels), F32),
            ((size.cells, channels), F32),
            ((2 * len(size.groups), lanes), F32),
        ],
        mid,
        queries,
        fine,
        gathered,
        wk,
        wv,
        mask,
    )
    out = call(
        functools.partial(last_kernel, size),
        [((size.cells, channels), BF16)],
        flat,
        gain_mlp,
        *late,
        queries,
        mid,
        got_a,
        got_b,
        coarse_out,
        fine_out,
        stats,
        wk,
        wv,
        mask,
        arrange,
        spaces=[hbm] * 5 + [vmem] * 11,
        scratch=[
            pltpu.VMEM((size.parts, size.mid_rows, LANES), F32),
            pltpu.VMEM((size.cells, channels), BF16),
            pltpu.VMEM((size.cells, channels), F32),
            pltpu.VMEM((2 * size.cells, lanes), BF16),
            pltpu.VMEM(flat.shape, BF16),
            pltpu.VMEM(gain_mlp.shape, F32),
            *[pltpu.VMEM(a.shape, BF16) for a in late],
            pltpu.SemaphoreType.DMA((5,)),
        ],
        vmem=False,
    )[0]
    return out.reshape(tokens.shape)


def solution(mesh):
    in_specs = (P("gx", "gy", "gz", None), P(), P(), P(), P(), P(), P(), P(), P(), P())
    out_specs = P("gx", "gy", "gz", None)
    return jax.shard_map(shards, mesh=mesh, in_specs=in_specs, out_specs=out_specs, check_vma=False)
```

```python
import functools
import math

import jax
import jax.numpy as jnp
import numpy as np
from jax import lax
from jax.experimental import pallas as pl
from jax.experimental.pallas import tpu as pltpu
from jax.sharding import PartitionSpec as P

HEADS = 8
EPSILON = 1e-05
LOG2E = 1.4426950408889634
NEGATIVE = -1e30
LANES = 128
F32 = jnp.float32
BF16 = jnp.bfloat16
AXES = ("gx", "gy", "gz")


def up_to(count, step):
    return -(-count // step) * step


def layer_norm(values, gain):
    average = jnp.mean(values, axis=-1, keepdims=True)
    centered = values - average
    variance = jnp.mean(centered * centered, axis=-1, keepdims=True)
    return (centered * lax.rsqrt(variance + EPSILON) * gain).astype(BF16)


def dot(left, right):
    return jnp.dot(left, right, preferred_element_type=F32)


def dot_nt(left, right):
    return lax.dot_general(left, right, (((1,), (1,)), ((), ())), preferred_element_type=F32)


def dot_tn(left, right):
    return lax.dot_general(left, right, (((0,), (0,)), ((), ())), preferred_element_type=F32)


def joined(ref, rows):
    return jnp.concatenate([ref[j, rows, :] for j in range(ref.shape[0])], axis=1)


def split_store(ref, rows, values):
    for j in range(ref.shape[0]):
        ref[j, rows, :] = values[:, j * LANES : (j + 1) * LANES]


def call(kernel, outs, *args, spaces=None, scratch=(), vmem=True, aliases=None, limit=24 << 20, work=None):
    kinds = [pltpu.VMEM(s, d) if vmem else jax.ShapeDtypeStruct(s, d) for s, d in outs]
    spaces = spaces or [pltpu.VMEM] * len(args)
    return pl.pallas_call(
        kernel,
        out_shape=kinds,
        in_specs=[pl.BlockSpec(memory_space=s) for s in spaces],
        out_specs=[pl.BlockSpec(memory_space=pltpu.VMEM) for _ in outs],
        scratch_shapes=list(scratch),
        input_output_aliases=aliases or {},
        compiler_params=pltpu.CompilerParams(vmem_limit_bytes=limit),
        cost_estimate=work and pl.CostEstimate(flops=work, bytes_accessed=0, transcendentals=0),
    )(*args)


class Sizes:
    def __init__(self, extent, channels):
        self.x, self.y, self.z = extent
        self.c = channels
        self.parts = channels // LANES
        self.cells = self.x * self.y * self.z
        self.mx, self.my, self.mz = (n // 2 for n in extent)
        self.mids = self.mx * self.my * self.mz
        self.coarse = self.mids // 8
        self.mzp = up_to(self.mz + 2, 8)
        self.fine_rows = (self.x + 2) * (self.y + 2) * self.z
        self.mid_rows = (self.mx + 2) * (self.my + 2) * self.mzp
        self.bias_rows = up_to(self.z + self.mzp + 2, 8)
        self.ones_at = self.mid_rows + self.bias_rows
        self.scale_at = self.ones_at + 4 * self.z
        self.kept_rows = self.scale_at + 8
        self.fy, self.gy = self.x * self.z, self.mx * self.mz
        self.fx, self.gx = (self.y + 2) * self.z, (self.my + 2) * self.mz
        self.fz, self.gz = (self.x + 2) * (self.y + 2), (self.mx + 2) * (self.my + 2)
        self.fzp, self.gzp = self.fz, self.gz
        self.groups = [(bx, by) for bx in range(self.x // 2) for by in range(self.y // 2)]
        self.group = 4 * self.z

    def query_rows(self, bx, by):
        return [
            slice(((2 * bx + dx) * self.y + 2 * by) * self.z, ((2 * bx + dx) * self.y + 2 * by + 2) * self.z)
            for dx in (0, 1)
        ]


def pooling(size):
    x, y, z = np.unravel_index(np.arange(size.cells), (size.x, size.y, size.z))
    middle = ((x // 2) * size.my + y // 2) * size.mz + z // 2
    coarse = ((x // 4) * (size.my // 2) + y // 4) * (size.mz // 2) + z // 4
    rows = np.zeros((size.mids + size.coarse, size.cells), np.float32)
    rows[middle, np.arange(size.cells)] = 1.0
    rows[size.mids + coarse, np.arange(size.cells)] = 1.0
    grid = rows[: size.mids].reshape(size.mx, size.my, size.mz, size.cells)
    faces = [grid[:, at].reshape(size.gy, size.cells) for at in (0, size.my - 1)]
    return np.concatenate([rows, rows[size.mids :], *faces]).astype(jnp.bfloat16)


def window_bias(size):
    query_z = np.arange(size.group) % size.z

    def seen(keys, factor):
        start = 2 * (query_z // factor)
        return (keys[:, None] >= start - 1) & (keys[:, None] <= start + 2)

    place = np.arange(size.mzp)
    middle = np.where(place < size.mz, place, np.where(place == size.mz, -1, size.mz))
    held = seen(middle, 4) & (place[:, None] < size.mz + 2)
    rows = np.concatenate([seen(np.arange(size.z), 2), held, seen(np.array([-1, size.z]), 2)])
    bias = np.where(rows, 0.0, NEGATIVE).astype(np.float32)
    bias = np.concatenate([bias, np.zeros((up_to(len(bias), 8) - len(bias), size.group), np.float32)])
    rows = np.tile(np.concatenate([bias, np.eye(size.group, dtype=np.float32)]), (1, HEADS))
    return np.ascontiguousarray(rows.reshape(len(rows), -1, LANES).transpose(1, 0, 2))


def arranging(size):
    rows = np.zeros((len(size.groups) * 32, 2 * size.fzp), np.float32)
    at = 0
    for bx, by in size.groups:
        for side in range(2):
            for kx in range(4):
                for ky in range(4):
                    rows[at, side * size.fzp + (2 * bx + kx) * (size.y + 2) + 2 * by + ky] = 1.0
                    at += 1
    return rows.astype(jnp.bfloat16)


def head_mask(size):
    head = np.arange(HEADS * size.group) // size.group
    return (head[:, None] == np.arange(size.c)[None, :] // (size.c // HEADS)).astype(jnp.bfloat16)


def fetch(sources, targets, sems):
    copies = [pltpu.make_async_copy(s, t, sems.at[i]) for i, (s, t) in enumerate(zip(sources, targets))]
    for copy in copies:
        copy.start()
    return copies


def is_odd(axis):
    return lax.axis_index(axis) % 2 == 1


def first_kernel(size, devices, tokens, gain, pool, both, faces, coarse_out, cells, gain_here, pool_here, sems):
    copies = fetch((tokens, gain, pool), (cells, gain_here, pool_here), sems)
    for copy in copies[:2]:
        copy.wait()
    values = layer_norm(cells[...].astype(F32), gain_here[...])
    both[: size.cells, :] = values
    copies[2].wait()
    pooled = dot(pool_here[...], values)
    at = size.mids + 2 * size.coarse
    both[size.cells :, :] = (pooled[: size.mids] * 0.125).astype(BF16)
    pack = (pooled[size.mids : at] * (1.0 / 64.0)).astype(BF16)
    for row in range(0, devices * size.coarse, 2 * size.coarse):
        coarse_out[row : row + 2 * size.coarse, :] = pack
    face = size.fy + size.gy
    for side, y in enumerate((0, size.y - 1)):
        rows = [slice((x * size.y + y) * size.z, (x * size.y + y + 1) * size.z) for x in range(size.x)]
        cut = jnp.concatenate([values[r].astype(F32) for r in rows], axis=0)
        faces[side * face : side * face + size.fy, :] = cut.astype(BF16)
        mids = pooled[at + side * size.gy : at + (side + 1) * size.gy] * 0.125
        faces[side * face + size.fy : (side + 1) * face, :] = mids.astype(BF16)


def prepare_kernel(size, both, after, biases, head_scale, *refs):
    held = (len(refs) - 5) // 2
    sources, targets = refs[:held], refs[held : 2 * held]
    queries, fine, mid, scale_here, sems = refs[2 * held :]
    rows = mid.at[:, pl.ds(size.mid_rows, size.scale_at - size.mid_rows), :]
    copies = fetch((*sources, head_scale, biases), (*targets, scale_here, rows), sems)
    cells = both[: size.cells, :].astype(F32)
    mids = both[size.cells :, :].astype(F32)
    mid[:, : size.mid_rows, :] = jnp.zeros((size.parts, size.mid_rows, LANES), F32)
    for x in range(size.x):
        at = ((x + 1) * (size.y + 2) + 1) * size.z
        split_store(fine, slice(at, at + size.y * size.z), cells[x * size.y * size.z : (x + 1) * size.y * size.z])
    for x in range(size.mx):
        for y in range(size.my):
            at = ((x + 1) * (size.my + 2) + y + 1) * size.mzp
            row = (x * size.my + y) * size.mz
            split_store(mid, slice(at, at + size.mz), mids[row : row + size.mz])
    copies[0].wait()
    queries[...] = dot(both[: size.cells, :], targets[0][...]).astype(BF16)
    for copy in copies[1:]:
        copy.wait()
    split_store(mid, slice(size.scale_at, size.scale_at + 1), lane_scale(size, scale_here))


def pick(odd, from_a, from_b):
    first, second = from_a[...].astype(F32), from_b[...].astype(F32)
    return jnp.where(odd, first, second), jnp.where(odd, second, first)


def from_sides(size, y_refs):
    if len(y_refs) == 1:
        both = y_refs[0][...].astype(F32)
        return both[size.fy + size.gy :], both[: size.fy + size.gy]
    return y_refs[0][...].astype(F32), y_refs[1][...].astype(F32)


def x_kernel(size, both, *refs):
    y_refs, (face_a, face_b) = refs[:-2], refs[-2:]
    y_low, y_high = from_sides(size, y_refs)
    cells = both[: size.cells, :].astype(F32)
    mids = both[size.cells :, :].astype(F32)

    def cut(x, mx):
        fine_at, own = slice(x * size.z, (x + 1) * size.z), size.y * size.z
        mid_at, own_mid = slice(size.fy + mx * size.mz, size.fy + (mx + 1) * size.mz), size.my * size.mz
        return jnp.concatenate(
            [
                y_low[fine_at],
                cells[x * own : (x + 1) * own],
                y_high[fine_at],
                y_low[mid_at],
                mids[mx * own_mid : (mx + 1) * own_mid],
                y_high[mid_at],
            ],
            axis=0,
        )

    low, high = cut(0, 0), cut(size.x - 1, size.mx - 1)
    odd = is_odd("gx")
    face_a[...] = jnp.where(odd, low, high).astype(BF16)
    face_b[...] = jnp.where(odd, high, low).astype(BF16)


def z_kernel(size, fine_in, mid_in, from_a, from_b, *refs):
    y_refs, (face_a, face_b, fine, mid) = refs[:-4], refs[-4:]
    y_low, y_high = from_sides(size, y_refs)
    low, high = pick(is_odd("gx"), from_a, from_b)
    for x, halo in ((0, low), (size.x + 1, high)):
        split_store(fine, slice(x * size.fx, (x + 1) * size.fx), halo[: size.fx])
    for x, halo in ((0, low), (size.mx + 1, high)):
        for y in range(size.my + 2):
            at = (x * (size.my + 2) + y) * size.mzp
            row = size.fx + y * size.mz
            split_store(mid, slice(at, at + size.mz), halo[row : row + size.mz])
    for y, my, halo in ((0, 0, y_low), (size.y + 1, size.my + 1, y_high)):
        for x in range(size.x):
            at = ((x + 1) * (size.y + 2) + y) * size.z
            split_store(fine, slice(at, at + size.z), halo[x * size.z : (x + 1) * size.z])
        for x in range(size.mx):
            at = ((x + 1) * (size.my + 2) + my) * size.mzp
            row = size.fy + x * size.mz
            split_store(mid, slice(at, at + size.mz), halo[row : row + size.mz])

    def cut(z, mz):
        parts = [
            joined(fine, pl.ds(z, size.fz, stride=size.z)),
            jnp.zeros((size.fzp - size.fz, size.c), F32),
            joined(mid, pl.ds(mz, size.gz, stride=size.mzp)),
            jnp.zeros((size.gzp - size.gz, size.c), F32),
        ]
        return jnp.concatenate([p for p in parts if p.shape[0]], axis=0)

    below, above = cut(0, 0), cut(size.z - 1, size.mz - 1)
    odd = is_odd("gz")
    face_a[...] = jnp.where(odd, below, above).astype(BF16)
    face_b[...] = jnp.where(odd, above, below).astype(BF16)


def lane_scale(size, head_scale):
    factor = LOG2E / math.sqrt(size.c // HEADS)
    return jnp.concatenate([jnp.full((1, size.group), head_scale[h] * factor, F32) for h in range(HEADS)], axis=1)


def spread_queries(size, queries, rows, mask):
    some = jnp.concatenate([queries[r, :] for r in rows], axis=0)
    return jnp.concatenate([some] * HEADS, axis=0) * mask


def soft(scores):
    weights = jnp.exp2(scores - jnp.max(scores, axis=0, keepdims=True))
    return (weights * (1.0 / jnp.sum(weights, axis=0, keepdims=True))).astype(BF16)


def tiled(scores, one):
    length = one.shape[0]
    return (scores.reshape(-1, length, scores.shape[-1]) + one[None]).reshape(scores.shape)


def gather_heads(size, total):
    heads, width = HEADS // size.parts, size.c // HEADS
    lane = lax.broadcasted_iota(jnp.int32, (size.group, LANES), 1)
    parts = []
    for j in range(size.parts):
        blocks = [
            total[(j * heads + h) * size.group : (j * heads + h + 1) * size.group, j * LANES : (j + 1) * LANES]
            for h in range(heads)
        ]
        result = blocks[0]
        for h in range(1, heads):
            result = jnp.where(lane >= h * width, blocks[h], result)
        parts.append(result)
    return jnp.concatenate(parts, axis=1)


def own_kernel(
    size, kept, queries, fine, coarse, key_weight, value_weight, mask, *refs
):
    late = (len(refs) - 4) // 2
    sources, (coarse_out, fine_out, stats, *targets), sems = refs[:late], refs[late:-1], refs[-1]
    copies = fetch(sources, targets, sems)
    block = joined(fine, slice(None)).astype(BF16)
    keys = dot(block, key_weight[...]).astype(BF16)
    values = dot(block, value_weight[...]).astype(BF16)
    cells = coarse[...]
    coarse_keys = dot(cells, key_weight[...]).astype(BF16)
    coarse_values = dot(cells, value_weight[...]).astype(BF16)
    scale = joined(kept, slice(size.scale_at, size.scale_at + 1))
    spread_mask = mask[...]
    run_bias = joined(kept, slice(size.mid_rows, size.mid_rows + size.z))
    fine_row = (size.y + 2) * size.z
    for index, (bx, by) in enumerate(size.groups):
        at = slice(index * size.group, (index + 1) * size.group)
        spread = spread_queries(size, queries, size.query_rows(bx, by), spread_mask)
        total = dot_tn(soft(dot_nt(coarse_keys, spread) * scale), coarse_values)
        coarse_out[at, :] = gather_heads(size, total)
        slabs = [
            slice((2 * bx + k) * fine_row + 2 * by * size.z, (2 * bx + k) * fine_row + (2 * by + 4) * size.z)
            for k in range(4)
        ]
        some_keys = jnp.concatenate([keys[s] for s in slabs], axis=0)
        some_values = jnp.concatenate([values[s] for s in slabs], axis=0)
        scores = tiled(dot_nt(some_keys, spread) * scale, run_bias)
        highest = jnp.max(scores, axis=0, keepdims=True)
        weights = jnp.exp2(scores - highest)
        stats[index : index + 1, :] = highest
        stats[len(size.groups) + index : len(size.groups) + index + 1, :] = jnp.sum(weights, axis=0, keepdims=True)
        fine_out[at, :] = gather_heads(size, dot_tn(weights.astype(BF16), some_values))
    for copy in copies:
        copy.wait()


def weigh_heads(size, total, wide):
    heads = HEADS // size.parts
    parts = []
    for j in range(size.parts):
        rows = slice(j * heads * size.group, (j + 1) * heads * size.group)
        cut = total[rows, j * LANES : (j + 1) * LANES].reshape(heads, size.group, LANES)
        parts.append(jnp.sum(cut * wide[:heads, :, :LANES], axis=0))
    return jnp.concatenate(parts, axis=1)


def last_kernel(
    size,
    mlp_gain,
    queries,
    mid_in,
    from_a,
    from_b,
    coarse_out,
    fine_out,
    stats,
    key_weight,
    value_weight,
    mask,
    arrange,
    tokens_here,
    out_here,
    up_here,
    down_here,
    out,
    mid,
    attended,
    joint,
    factors,
    gain_here,
    sems,
):
    copies = fetch((mlp_gain,), (gain_here,), sems)
    low, high = pick(is_odd("gz"), from_a, from_b)
    mid[...] = mid_in[:, : size.mid_rows, :]
    split_store(mid, pl.ds(size.mz, size.gz, stride=size.mzp), low[size.fzp : size.fzp + size.gz])
    split_store(mid, pl.ds(size.mz + 1, size.gz, stride=size.mzp), high[size.fzp : size.fzp + size.gz])
    ends = jnp.concatenate([low[: size.fzp], high[: size.fzp]], axis=0).astype(BF16)
    ends = dot(arrange[...], ends).astype(BF16)
    mids = joined(mid, slice(None)).astype(BF16)
    cells = jnp.concatenate([ends, mids], axis=0)
    keys = dot(cells, key_weight[...]).astype(BF16)
    values = dot(cells, value_weight[...]).astype(BF16)
    scale = joined(mid_in, slice(size.scale_at, size.scale_at + 1))
    spread_mask = mask[...]
    wide = spread_mask.astype(F32).reshape(HEADS, size.group, size.c)
    bias = joined(mid_in, slice(size.mid_rows + size.z, size.ones_at))
    mid_bias, low_bias, high_bias = bias[: size.mzp], bias[size.mzp : size.mzp + 1], bias[size.mzp + 1 : size.mzp + 2]
    ones = joined(mid_in, slice(size.ones_at, size.scale_at))
    mid_row = (size.my + 2) * size.mzp
    count = len(size.groups)

    for index, (bx, by) in enumerate(size.groups):
        at = slice(index * size.group, (index + 1) * size.group)
        spread = spread_queries(size, queries, size.query_rows(bx, by), spread_mask)
        ends_at = slice(32 * index, 32 * index + 32)
        start = [
            count * 32 + (2 * (bx // 2) + k) * mid_row + 2 * (by // 2) * size.mzp for k in range(4)
        ]
        slabs = [ends_at] + [slice(s, s + 4 * size.mzp) for s in start]
        both = dot_nt(jnp.concatenate([keys[s] for s in slabs], axis=0), spread) * scale
        scores = jnp.concatenate([both[:16] + low_bias, both[16:32] + high_bias], axis=0)
        before = stats[index : index + 1, :]
        highest = jnp.maximum(before, jnp.max(scores, axis=0, keepdims=True))
        weights = jnp.exp2(scores - highest)
        shrink = jnp.exp2(before - highest)
        summed = stats[count + index : count + index + 1, :] * shrink + jnp.sum(weights, axis=0, keepdims=True)
        inverse = 1.0 / summed
        factor = ones * (shrink * inverse)
        coarser = factor.astype(BF16)
        factors[at, :] = coarser
        finer = slice(count * size.group + at.start, count * size.group + at.stop)
        factors[finer, :] = (factor - coarser.astype(F32)).astype(BF16)
        weights = jnp.concatenate([(weights * inverse).astype(BF16), soft(tiled(both[32:], mid_bias))], axis=0)
        total = dot_tn(weights, jnp.concatenate([values[s] for s in slabs], axis=0))
        joint[at, :] = weigh_heads(size, total, wide) + coarse_out[at, :]

    spread_factors = dot(factors[...], spread_mask)
    half = count * size.group
    result = joint[...] + fine_out[...] * (spread_factors[:half] + spread_factors[half:])
    for index, (bx, by) in enumerate(size.groups):
        part = result[index * size.group : (index + 1) * size.group].astype(BF16)
        for k, r in enumerate(size.query_rows(bx, by)):
            attended[r, :] = part[k * 2 * size.z : (k + 1) * 2 * size.z]
    for copy in copies:
        copy.wait()
    residual = (tokens_here[...].astype(F32) + dot(attended[...], out_here[...])).astype(BF16)
    second = layer_norm(residual.astype(F32), gain_here[...])
    hidden = jax.nn.gelu(dot(second, up_here[...]), approximate=True).astype(BF16)
    out[...] = (residual.astype(F32) + dot(hidden, down_here[...])).astype(BF16)


def swap(array, axis, start):
    count = lax.axis_size(axis)
    pairs = []
    for i in range(start, count, 2):
        other = (i + 1) % count
        pairs += [(i, other), (other, i)]
    return lax.ppermute(array, axis, pairs)


def shift(array, axis, by):
    count = lax.axis_size(axis)
    return lax.ppermute(array, axis, [(i, (i + by) % count) for i in range(count)])


def shards(
    tokens,
    norm_gain,
    query_weight,
    key_weight,
    value_weight,
    head_scale,
    out_weight,
    mlp_gain,
    up_weight,
    down_weight,
):
    channels = tokens.shape[-1]
    size = Sizes(tokens.shape[:3], channels)
    devices = math.prod(lax.axis_size(a) for a in AXES)
    fx, gx, fy, gy = size.fx, size.gx, size.fy, size.gy
    face_z = size.fzp + size.gzp
    smem, vmem, hbm = pltpu.SMEM, pltpu.VMEM, pltpu.HBM

    def pinned(*arrays):
        return [pltpu.with_memory_space_constraint(jnp.asarray(a), hbm) for a in arrays]

    flat, gain, gain_mlp, scales = pinned(
        tokens.reshape(size.cells, channels), norm_gain.reshape(1, -1), mlp_gain.reshape(1, -1), head_scale
    )
    biases, pool = pinned(window_bias(size), pooling(size))
    both, faces, coarse = call(
        functools.partial(first_kernel, size, devices),
        [
            ((size.cells + size.mids, channels), BF16),
            ((2 * (fy + gy), channels), BF16),
            ((devices * size.coarse, channels), BF16),
        ],
        flat,
        gain,
        pool,
        spaces=[hbm] * 3,
        scratch=[
            pltpu.VMEM(flat.shape, BF16),
            pltpu.VMEM(gain.shape, F32),
            pltpu.VMEM(pool.shape, BF16),
            pltpu.SemaphoreType.DMA((3,)),
        ],
    )
    if lax.axis_size("gy") == 2:
        from_y = [swap(faces, "gy", 0)]
    else:
        from_y = [shift(faces[fy + gy :], "gy", 1), shift(faces[: fy + gy], "gy", -1)]
    gathered = lax.all_to_all(coarse.reshape(devices, size.coarse, channels), AXES, 0, 0).reshape(-1, channels)
    face_a, face_b = call(
        functools.partial(x_kernel, size),
        [((fx + gx, channels), BF16), ((fx + gx, channels), BF16)],
        both,
        *from_y,
        work=20_000_000_000,
    )
    from_a = swap(face_a, "gx", 0)
    from_b = swap(face_b, "gx", 1)
    held = pinned(
        query_weight,
        key_weight,
        value_weight,
        head_mask(size),
        arranging(size),
    )
    late = pinned(out_weight, up_weight, down_weight)
    *weights, queries, fine, mid = call(
        functools.partial(prepare_kernel, size),
        [(a.shape, a.dtype) for a in held]
        + [
            ((size.cells, channels), BF16),
            ((size.parts, size.fine_rows, LANES), F32),
            ((size.parts, size.kept_rows, LANES), F32),
        ],
        both,
        face_a,
        biases,
        scales,
        *held,
        spaces=[vmem] * 2 + [hbm] * (2 + len(held)),
        scratch=[pltpu.SMEM((HEADS,), F32), pltpu.SemaphoreType.DMA((2 + len(held),))],
    )
    wq, wk, wv, mask, arrange = weights
    z_a, z_b, fine, mid = call(
        functools.partial(z_kernel, size),
        [
            ((face_z, channels), BF16),
            ((face_z, channels), BF16),
            ((size.parts, size.fine_rows, LANES), F32),
            ((size.parts, size.kept_rows, LANES), F32),
        ],
        fine,
        mid,
        from_a,
        from_b,
        *from_y,
        aliases={0: 2, 1: 3},
    )
    got_a = swap(z_a, "gz", 0)
    got_b = swap(z_b, "gz", 1)
    lanes = HEADS * size.group
    late = [flat, *late]
    coarse_out, fine_out, stats, *late_here = call(
        functools.partial(own_kernel, size),
        [
            ((size.cells, channels), F32),
            ((size.cells, channels), F32),
            ((2 * len(size.groups), lanes), F32),
        ]
        + [(a.shape, a.dtype) for a in late],
        mid,
        queries,
        fine,
        gathered,
        wk,
        wv,
        mask,
        *late,
        spaces=[vmem] * 7 + [hbm] * len(late),
        scratch=[pltpu.SemaphoreType.DMA((len(late),))],
    )
    out = call(
        functools.partial(last_kernel, size),
        [((size.cells, channels), BF16)],
        gain_mlp,
        queries,
        mid,
        got_a,
        got_b,
        coarse_out,
        fine_out,
        stats,
        wk,
        wv,
        mask,
        arrange,
        *late_here,
        spaces=[hbm] + [vmem] * 15,
        scratch=[
            pltpu.VMEM((size.parts, size.mid_rows, LANES), F32),
            pltpu.VMEM((size.cells, channels), BF16),
            pltpu.VMEM((size.cells, channels), F32),
            pltpu.VMEM((2 * size.cells, lanes), BF16),
            pltpu.VMEM(gain_mlp.shape, F32),
            pltpu.SemaphoreType.DMA((1,)),
        ],
        vmem=False,
    )[0]
    return out.reshape(tokens.shape)


def solution(mesh):
    in_specs = (P("gx", "gy", "gz", None), P(), P(), P(), P(), P(), P(), P(), P(), P())
    out_specs = P("gx", "gy", "gz", None)
    return jax.shard_map(shards, mesh=mesh, in_specs=in_specs, out_specs=out_specs, check_vma=False)
```
